32 devices in a mesh: group: 8 (over z, core), mp: 4 (over y, x).
Axes of the slice: x: 2, y: 2, z: 4, core: 2. Of those that a mesh axis runs over, the one named last changes fastest.
Arguments:
- captions: bfloat16 [2048, 4096], P('group', 'mp'), may hold values from -6 to 6
- key_weight: bfloat16 [4096, 6144], P(None, 'mp'), may hold values from -0.09375 to 0.09375
- value_weight: bfloat16 [4096, 6144], P(None, 'mp'), may hold values from -0.09375 to 0.09375
- queries: bfloat16 [4096, 6144], P('group', 'mp'), may hold values from -400 to 400
- tile_clip: int32 [512, 1], P('group'), may hold values from 0 to 7; in each aligned block of 64 rows (0 to 63, 64 to 127, ...) at most 16 rows name the same one
- tile_length: int32 [512], P('group'), may hold values from 2 to 4, as said below
Outputs:
- attended: bfloat16 [4096, 6144], P('group', 'mp')
The draws below stay inside these ranges and needn't reach their ends.
Inputs may be any that keep to these rules, and one draw needn't show every extreme that they name: `tile_clip`: among the tiles of one index of group at most 16 name the same clip, a bound that some block reaches of them; every clip is named by some tile. `tile_length`: the first tile of each index of group is full.
All inputs are finite; a program needn't handle non-finite values.
Results may differ from the reference program's by a relative error of at most 0.011.
Values may be sent and summed in bfloat16 or wider, within the bound.
A program may use at most 128 MiB of HBM per device.

```python
import math
import jax
import jax.numpy as jnp
import numpy as np
from jax import lax

D_ENC = 4096
HEADS = 48
HEAD_DIM = 128
TILE = 4
VID_ROWS = 512
TILES_DEV = 64
SLOT = 16
ENC_ROWS = 256
N_GROUP = 8


def draw_queries(key, part):
    first = jax.random.fold_in(jax.random.fold_in(key, 7), 0)
    rows = N_GROUP * VID_ROWS
    base = jax.random.normal(first, (rows, HEADS * HEAD_DIM), jnp.float32)
    base = jnp.clip(base, -6.0, 6.0)
    return base.astype(jnp.bfloat16)


def draw_tile_length(key, part):
    low = (TILE + 1) // 2
    drawn = jax.random.randint(jax.random.fold_in(key, 11), (N_GROUP * TILES_DEV,), low, TILE + 1)
    first = jnp.arange(N_GROUP * TILES_DEV) % TILES_DEV == 0
    return jnp.where(first, TILE, drawn).astype(jnp.int32)


def levels(own_key, dims, cuts, low, high):
    def one(dim, shards_of):
        steps = jax.random.uniform(jax.random.fold_in(jax.random.fold_in(own_key, 6), dim), (shards_of,), jnp.float32, low / len(cuts), high / len(cuts))
        return jnp.repeat(jnp.exp(steps), dims[dim] // shards_of).reshape((-1,) + (1,) * (len(dims) - dim - 1))

    factor_of = one(*cuts[0])
    for cut in cuts[1:]:
        factor_of = factor_of * one(*cut)
    return factor_of


def deal_out(rng, own, number, rows, number_of, top, limit, slope):
    ranking = jax.random.permutation(rng, number_of)
    crowded, common = portions_of(number_of, rows * top, limit, slope, True), portions_of(number_of, rows * top, limit, slope, False)
    places = jnp.arange(number_of)

    def named(tallies, offset_by):
        used = int((tallies > 0).sum())
        fixed = max(1, used // 4)
        passed = fixed + (places - fixed + offset_by * (used - fixed)) % max(1, number_of - fixed)
        return jnp.zeros((number_of,), jnp.int32).at[ranking[jnp.where(places < fixed, places, passed)]].set(jnp.asarray(tallies, jnp.int32))

    tallies = jnp.where(number % 4 == 0, named(crowded, number // 4), named(common, number - number // 4 - 1))
    mixed = jax.random.permutation(jax.random.fold_in(own, 3), number_of)
    source_of, receiver = mixed[0:number_of // 2 * 2:2], mixed[1:number_of // 2 * 2:2]
    slack = jnp.minimum(tallies[source_of] - 1, limit - tallies[receiver]) // 2
    slack = jnp.where((source_of == ranking[0]) | (receiver == ranking[0]) | (tallies[receiver] == 0), 0, jnp.maximum(slack, 0))
    passed = jax.random.randint(jax.random.fold_in(own, 4), (number_of // 2,), 0, 1 << 20) % (slack + 1)
    tallies = tallies.at[source_of].add(-passed).at[receiver].add(passed)
    items = jnp.searchsorted(jnp.cumsum(tallies), jnp.arange(rows * top), side="right").astype(jnp.int32)
    grid = items.reshape(top, rows).T
    grid = grid[jax.random.permutation(jax.random.fold_in(own, 1), rows)]
    offset_by = jax.random.randint(jax.random.fold_in(own, 2), (rows, 1), 0, top)
    return jnp.take_along_axis(grid, (jnp.arange(top)[None, :] + offset_by) % top, axis=1)


def portions_of(count, total, bound, slope, full):
    portions = [(1 << 20) // math.isqrt(standing ** slope) + 1 for standing in range(1, count + 1)]
    largest = bound if full else min(bound, max(-(-total // count), total * portions[0] // sum(portions)))
    least = 1 if total - largest >= count - 1 else 0
    holding, spare = [largest] + [least] * (count - 1), total - largest - least * (count - 1)
    while spare > 0:
        free = [i for i in range(1, count) if holding[i] < largest] or [i for i in range(1, count) if holding[i] < bound]
        mass, left = sum([portions[i] for i in free]), spare
        for i in free:
            extra = min(bound - holding[i], max(1, left * portions[i] // mass), spare)
            holding[i] = holding[i] + extra
            spare = spare - extra
    return np.array(holding)


def centred(key, dims, deviation, limit, cuts=(), kind=jnp.bfloat16):
    array = jax.random.normal(key, dims, jnp.float32) * deviation
    if len(cuts) > 0:
        array = levels(key, dims, cuts, -0.22, 0.18) * array
    return jnp.clip(array, min=-limit, max=limit).astype(kind)


def setup_inputs(seed: int = 0) -> dict:
    streams_of = jax.random.split(jax.random.key(seed), 7)
    captions = centred(streams_of[0], (N_GROUP * ENC_ROWS, D_ENC), 1.0, 6.0, ((0, 8), (1, 4)))
    key_weight = centred(streams_of[1], (D_ENC, HEADS * HEAD_DIM), D_ENC ** -0.5, 0.09375, ((1, 4),))
    value_weight = centred(streams_of[2], (D_ENC, HEADS * HEAD_DIM), D_ENC ** -0.5, 0.09375, ((1, 4),))
    queries = draw_queries(jax.random.fold_in(streams_of[6], 71), 0)
    tile_clip_keys = jax.random.split(jax.random.fold_in(streams_of[4], 1), (N_GROUP * TILES_DEV) // TILES_DEV)
    tile_clip_turns = jax.random.permutation(jax.random.fold_in(streams_of[4], 3), (N_GROUP * TILES_DEV) // TILES_DEV)
    tile_clip = jax.vmap(lambda own, number: deal_out(jax.random.fold_in(streams_of[4], 2), own, number, TILES_DEV, N_GROUP, 1, SLOT, 1))(tile_clip_keys, tile_clip_turns).reshape((N_GROUP * TILES_DEV, 1))
    tile_length = draw_tile_length(jax.random.fold_in(streams_of[6], 71), 0)
    return dict(captions=captions, key_weight=key_weight, value_weight=value_weight, queries=queries, tile_clip=tile_clip, tile_length=tile_length)


def reference(captions, key_weight, value_weight, queries, tile_clip, tile_length):
    groups = N_GROUP
    slots = SLOT
    keys = jnp.dot(captions, key_weight, preferred_element_type=jnp.float32).astype(jnp.bfloat16)
    values = jnp.dot(captions, value_weight, preferred_element_type=jnp.float32).astype(jnp.bfloat16)
    target = tile_clip[:, 0].reshape(groups, TILES_DEV)
    onehot = (target[:, :, None] == jnp.arange(groups, dtype=jnp.int32)[None, None, :]).astype(jnp.int32)
    ranks = jnp.sum(jnp.cumsum(onehot, axis=1) * onehot, axis=2) - 1
    slot_of = target * slots + ranks
    match = slot_of[:, None, :] == jnp.arange(groups * slots, dtype=jnp.int32)[None, :, None]
    tile_index = jnp.sum(jnp.where(match, jnp.arange(TILES_DEV, dtype=jnp.int32)[None, None, :], 0), axis=2).astype(jnp.int32)
    filled = jnp.any(match, axis=2)
    global_tile = (jnp.arange(groups, dtype=jnp.int32)[:, None] * TILES_DEV + tile_index).astype(jnp.int32)
    slot_length = jnp.where(filled, tile_length[global_tile], 0).astype(jnp.int32)
    global_tile = global_tile.reshape(groups, groups, slots).transpose(1, 0, 2).reshape(groups, groups * slots)
    slot_length = slot_length.reshape(groups, groups, slots).transpose(1, 0, 2).reshape(groups, groups * slots)
    query_blocks = queries.reshape(groups, VID_ROWS, HEADS * HEAD_DIM)
    scale = 1.0 / (HEAD_DIM ** 0.5)

    def one_clip(items):
        tiles_here, lengths_here, query_here = items
        positions = jnp.arange(TILE, dtype=jnp.int32)
        rows = (tiles_here[:, None] * TILE + positions[None, :]).reshape(-1).astype(jnp.int32)
        live = (positions[None, :] < lengths_here[:, None]).reshape(-1)
        key_rows = keys[rows].reshape(-1, HEADS, HEAD_DIM).astype(jnp.float32)
        value_rows = values[rows].reshape(-1, HEADS, HEAD_DIM).astype(jnp.float32)
        query_heads = query_here.reshape(VID_ROWS, HEADS, HEAD_DIM).astype(jnp.float32)
        scores = jnp.einsum('qhd,khd->hqk', query_heads, key_rows) * scale
        scores = jnp.where(live[None, None, :], scores, jnp.float32(-1e30))
        top = jnp.max(scores, axis=2, keepdims=True)
        expo = jnp.where(live[None, None, :], jnp.exp(scores - top), jnp.float32(0.0))
        weights = (expo / jnp.sum(expo, axis=2, keepdims=True)).astype(jnp.bfloat16)
        output = jnp.einsum('hqk,khd->qhd', weights.astype(jnp.float32), value_rows)
        return output.reshape(VID_ROWS, HEADS * HEAD_DIM).astype(jnp.bfloat16)

    result = lax.map(one_clip, (global_tile, slot_length, query_blocks))
    return result.reshape(groups * VID_ROWS, HEADS * HEAD_DIM)
```

```python
import functools

import jax
import jax.numpy as jnp
from jax import lax
from jax.experimental import pallas as pl
from jax.experimental.pallas import tpu as pltpu
from jax.sharding import PartitionSpec as P

HEAD_DIM = 128
MESH = pl.DeviceIdType.MESH


def ring_place(i, n):
    half = n // 2
    far = i // half
    return i * (1 - far) + far * (n + half - 1 - i)


def offsets_of(groups):
    order = [0]
    for k in range(1, groups // 2 + 1):
        order.append(k)
        if groups - k != k:
            order.append(groups - k)
    return order


def widest(total, options):
    return next(o for o in options if total % o == 0)


def kernel(
    groups, n, rs, chunks, halves,
    slot_ref, cap_ref, kw_ref, vw_ref, q_hbm, out_ref,
    x, w, stage, live_stage, live, acc, q,
    w_sem, q_sem, z_send, z_recv, l_send, l_recv, r_send, r_recv,
):
    g = lax.axis_index("group")
    m = lax.axis_index("mp")
    place = ring_place(m, n)
    right = ring_place(lax.rem(place + 1, n), n)
    left = ring_place(lax.rem(place + n - 1, n), n)
    rows, width = stage.shape
    head_cols = kw_ref.shape[1]
    cols = 2 * head_cols
    hops = n // 2
    order = offsets_of(groups)

    def weight_copies(f):
        hop = (f + 1) // 2
        owner = ring_place(lax.rem(place + (n - hop if f % 2 else hop), n), n)
        part = pl.ds(pl.multiple_of(owner * width, width), width)
        return [
            pltpu.make_async_copy(kw_ref.at[part], w.at[f, :, pl.ds(0, head_cols)], w_sem.at[f, 0]),
            pltpu.make_async_copy(vw_ref.at[part], w.at[f, :, pl.ds(head_cols, head_cols)], w_sem.at[f, 1]),
        ]

    for f in range(n):
        for c in weight_copies(f):
            c.start()
    q_copy = pltpu.make_async_copy(q_hbm, q, q_sem)
    q_copy.start()

    barrier = pltpu.get_barrier_semaphore()
    for k in order[1:]:
        pl.semaphore_signal(barrier, inc=1, device_id=(lax.rem(g + k, groups), m), device_id_type=MESH)
    for side in (left, right):
        pl.semaphore_signal(barrier, inc=1, device_id=(g, side), device_id_type=MESH)

    tokens = cap_ref.shape[0]
    hit = lax.broadcasted_iota(jnp.int32, (rows, tokens), 0) == slot_ref[...]
    select = jnp.where(hit, 1.0, 0.0).astype(jnp.bfloat16)
    placed = jnp.dot(select, cap_ref[...], preferred_element_type=jnp.float32).astype(jnp.bfloat16)
    stage[...] = placed
    x[0, pl.ds(0, rs), :] = placed[:rs]
    flags = jnp.dot(
        select, jnp.ones((tokens, HEAD_DIM), jnp.bfloat16), preferred_element_type=jnp.float32
    ).astype(jnp.bfloat16)
    live_stage[...] = flags
    live[pl.ds(0, rs), :] = flags[:rs]

    pl.semaphore_wait(barrier, groups - 1 + 2)

    routes, flag_routes = [None], [None]
    for p in range(1, groups):
        part = pl.ds(p * rs, rs)
        to = (lax.rem(g + order[p], groups), m)
        routes.append(pltpu.make_async_remote_copy(
            src_ref=stage.at[part], dst_ref=x.at[0, part], send_sem=z_send.at[p],
            recv_sem=z_recv.at[p], device_id=to, device_id_type=MESH))
        flag_routes.append(pltpu.make_async_remote_copy(
            src_ref=live_stage.at[part], dst_ref=live.at[part], send_sem=l_send.at[p],
            recv_sem=l_recv.at[p], device_id=to, device_id_type=MESH))

    chunk_rows = rows // chunks
    chunk_slots = groups // chunks

    def ring_copy(c, h, side):
        first, count = c * chunk_rows, chunk_rows
        if h == hops:
            count = chunk_rows // 2
            first = first + (count if side else 0)
        part = pl.ds(first, count)
        source = 0 if h == 1 else 2 * (h - 1) - 1 + side
        target = n - 1 if h == hops else 2 * h - 1 + side
        return pltpu.make_async_remote_copy(
            src_ref=x.at[source, part], dst_ref=x.at[target, part],
            send_sem=r_send.at[c, h - 1, side], recv_sem=r_recv.at[c, h - 1, side],
            device_id=(g, left if side else right), device_id_type=MESH)

    def hop(c, h):
        if h == 1:
            for p in range(c * chunk_slots, (c + 1) * chunk_slots):
                if p:
                    routes[p].wait_recv()
        else:
            ring_copy(c, h - 1, 0).wait_recv()
            ring_copy(c, h - 1, 1).wait_recv()
        ring_copy(c, h, 0).start()
        ring_copy(c, h, 1).start()

    half_rows = rows // halves
    half_chunks = chunks // halves
    tile = widest(cols, (512, 256, 128))
    seen = set()

    def project(part, f):
        if f not in seen:
            seen.add(f)
            for c in weight_copies(f):
                c.wait()
        if f == n - 1:
            for c in range(part * half_chunks, (part + 1) * half_chunks):
                ring_copy(c, hops, 0).wait_recv()
                ring_copy(c, hops, 1).wait_recv()
        span = pl.ds(part * half_rows, half_rows)

        def body(j, carry):
            at = pl.ds(pl.multiple_of(j * tile, tile), tile)
            term = jnp.dot(x[f, span, :], w[f, :, at], preferred_element_type=jnp.float32)
            if f == 0:
                acc[span, at] = term
            else:
                acc[span, at] += term
            return carry

        lax.fori_loop(0, cols // tile, body, 0)

    for p in range(1, groups):
        if p == 1:
            ring_copy(0, 1, 0).start() if chunk_slots == 1 else None
            ring_copy(0, 1, 1).start() if chunk_slots == 1 else None
        routes[p].start()
        flag_routes[p].start()

    ready = []
    for step in range(chunks + hops - 1):
        for h in range(1, hops + 1):
            c = step - (h - 1)
            if 0 <= c < chunks and not (c == 0 and h == 1 and chunk_slots == 1):
                hop(c, h)
        for part in range(halves):
            last = (part + 1) * half_chunks - 1
            if step == last:
                ready.append((part, 0))
            for h in range(1, hops):
                if step == last + h:
                    ready.extend([(part, 2 * h - 1), (part, 2 * h)])
            if step == last + hops - 1:
                ready.append((part, n - 1))
        if ready:
            project(*ready.pop(0))
    while ready:
        project(*ready.pop(0))

    q_copy.wait()
    for p in range(1, groups):
        flag_routes[p].wait_recv()

    flags_bf = live[...]
    bias = jnp.transpose((flags_bf.astype(jnp.float32) - 1.0) * 1e30)[0:1, :]
    factor = 1.4426950408889634 / HEAD_DIM**0.5
    q_rows = q.shape[0]
    q_tile = widest(q_rows, (256, 128, 64))

    def head(i, carry):
        kcol = pl.ds(pl.multiple_of(i * HEAD_DIM, HEAD_DIM), HEAD_DIM)
        vcol = pl.ds(pl.multiple_of(head_cols + i * HEAD_DIM, HEAD_DIM), HEAD_DIM)
        keys = acc[:, kcol].astype(jnp.bfloat16)
        values = jnp.concatenate([acc[:, vcol].astype(jnp.bfloat16), live[...]], axis=1)
        for t in range(q_rows // q_tile):
            at = pl.ds(t * q_tile, q_tile)
            scores = lax.dot_general(
                q[at, kcol], keys, (((1,), (1,)), ((), ())), preferred_element_type=jnp.float32
            ) + bias
            top = jnp.max(scores, axis=1, keepdims=True)
            weights = jnp.exp2((scores - top) * factor).astype(jnp.bfloat16)
            both = jnp.dot(weights, values, preferred_element_type=jnp.float32)
            out_ref[at, kcol] = (both[:, :HEAD_DIM] / both[:, HEAD_DIM:]).astype(out_ref.dtype)
        return carry

    lax.fori_loop(0, head_cols // HEAD_DIM, head, 0)

    for p in range(1, groups):
        routes[p].wait_send()
        flag_routes[p].wait_send()
    for c in range(chunks):
        for h in range(1, hops + 1):
            for side in (0, 1):
                ring_copy(c, h, side).wait_send()


def local(captions, key_weight, value_weight, queries, tile_clip, tile_length):
    groups, n = lax.axis_size("group"), lax.axis_size("mp")
    g = lax.axis_index("group")
    tiles = tile_length.shape[0]
    tokens, width = captions.shape
    tile = tokens // tiles
    slots = max(2, 2 * tiles // groups)
    rs = -(-slots * tile // 16) * 16
    rows = groups * rs
    chunks, halves = min(groups, 8), 2
    head_cols = key_weight.shape[1]

    clip = tile_clip[:, 0]
    index = jnp.arange(tiles, dtype=jnp.int32)
    before = (clip[None, :] == clip[:, None]) & (index[None, :] < index[:, None])
    rank = jnp.sum(before.astype(jnp.int32), axis=1)
    off = lax.rem(clip - g + groups, groups)
    slot = jnp.where(off == 0, 0, jnp.where(off <= groups // 2, 2 * off - 1, 2 * (groups - off)))
    first = slot * rs + rank * tile
    token = jnp.arange(tile, dtype=jnp.int32)
    at = jnp.where(token[None, :] < tile_length[:, None], first[:, None] + token[None, :], -1)
    at = at.reshape(1, tokens)

    hops = n // 2
    bf = jnp.bfloat16
    vmem = pl.BlockSpec(memory_space=pltpu.VMEM)
    hbm = pl.BlockSpec(memory_space=pl.ANY)
    dma = pltpu.SemaphoreType.DMA
    return pl.pallas_call(
        functools.partial(kernel, groups, n, rs, chunks, halves),
        out_shape=jax.ShapeDtypeStruct(queries.shape, bf),
        in_specs=[vmem, vmem, hbm, hbm, hbm],
        out_specs=vmem,
        scratch_shapes=[
            pltpu.VMEM((n, rows, width), bf),
            pltpu.VMEM((n, width, 2 * head_cols), bf),
            pltpu.VMEM((rows, width), bf),
            pltpu.VMEM((rows, HEAD_DIM), bf),
            pltpu.VMEM((rows, HEAD_DIM), bf),
            pltpu.VMEM((rows, 2 * head_cols), jnp.float32),
            pltpu.VMEM(queries.shape, bf),
            dma((n, 2)), dma(()),
            dma((groups,)), dma((groups,)), dma((groups,)), dma((groups,)),
            dma((chunks, hops, 2)), dma((chunks, hops, 2)),
        ],
        compiler_params=pltpu.CompilerParams(
            collective_id=0, has_side_effects=True, vmem_limit_bytes=58 * 1024 * 1024
        ),
        cost_estimate=pl.CostEstimate(
            flops=4 * rows * n * width * head_cols + 4 * queries.size * rows,
            bytes_accessed=4 * key_weight.size + 4 * queries.size,
            transcendentals=queries.size * rows // HEAD_DIM,
        ),
    )(at, captions, key_weight, value_weight, queries)


def solution(mesh):
    placed = (
        P("group", "mp"),
        P(None, "mp"),
        P(None, "mp"),
        P("group", "mp"),
        P("group", None),
        P("group"),
    )
    return jax.shard_map(
        local, mesh=mesh, in_specs=placed, out_specs=P("group", "mp"), check_vma=False
    )
```

```python
import functools

import jax
import jax.numpy as jnp
from jax import lax
from jax.experimental import pallas as pl
from jax.experimental.pallas import tpu as pltpu
from jax.sharding import PartitionSpec as P

HEAD_DIM = 128
MESH = pl.DeviceIdType.MESH


def ring_place(i, n):
    half = n // 2
    far = i // half
    return i * (1 - far) + far * (n + half - 1 - i)


def offsets_of(groups):
    order = [0]
    for k in range(1, groups // 2 + 1):
        order.append(k)
        if groups - k != k:
            order.append(groups - k)
    return order


def widest(total, options):
    return next(o for o in options if total % o == 0)


def kernel(
    groups, n, rs, chunks, halves,
    clip_ref, length_ref, cap_ref, kw_ref, vw_ref, q_hbm, out_ref,
    x, w, stage, live_stage, live, acc, q,
    w_sem, q_sem, z_send, z_recv, l_send, l_recv, r_send, r_recv,
):
    g = lax.axis_index("group")
    m = lax.axis_index("mp")
    place = ring_place(m, n)
    right = ring_place(lax.rem(place + 1, n), n)
    left = ring_place(lax.rem(place + n - 1, n), n)
    rows, width = stage.shape
    head_cols = kw_ref.shape[1]
    cols = 2 * head_cols
    hops = n // 2
    order = offsets_of(groups)

    def weight_copies(f):
        hop = (f + 1) // 2
        owner = ring_place(lax.rem(place + (n - hop if f % 2 else hop), n), n)
        part = pl.ds(pl.multiple_of(owner * width, width), width)
        return [
            pltpu.make_async_copy(kw_ref.at[part], w.at[f, :, pl.ds(0, head_cols)], w_sem.at[f, 0]),
            pltpu.make_async_copy(vw_ref.at[part], w.at[f, :, pl.ds(head_cols, head_cols)], w_sem.at[f, 1]),
        ]

    for f in range(n):
        for c in weight_copies(f):
            c.start()
    q_copy = pltpu.make_async_copy(q_hbm, q, q_sem)
    q_copy.start()

    barrier = pltpu.get_barrier_semaphore()
    for k in order[1:]:
        pl.semaphore_signal(barrier, inc=1, device_id=(lax.rem(g + k, groups), m), device_id_type=MESH)
    for side in (left, right):
        pl.semaphore_signal(barrier, inc=1, device_id=(g, side), device_id_type=MESH)

    f32, i32 = jnp.float32, jnp.int32
    tokens, tiles = cap_ref.shape[0], length_ref.shape[1]
    size = tokens // tiles
    row = lax.broadcasted_iota(i32, (tiles, tiles), 0)
    column = lax.broadcasted_iota(i32, (tiles, tiles), 1)
    def upright(across):
        return jnp.sum(jnp.where(row == column, across, 0.0), axis=1, keepdims=True)

    clip_across = clip_ref[...].astype(f32)
    clip = upright(clip_across)
    length = upright(length_ref[...].astype(f32))
    rank = jnp.sum(
        jnp.where((clip == clip_across) & (column < row), 1.0, 0.0), axis=1, keepdims=True
    )
    off = clip.astype(i32) - g
    off = jnp.where(off < 0, off + groups, off)
    slot = jnp.where(off == 0, 0, jnp.where(off <= groups // 2, 2 * off - 1, 2 * (groups - off)))
    first = slot.astype(f32) * rs + rank * size
    part_of = lax.broadcasted_iota(i32, (tiles, tokens), 1) - size * lax.broadcasted_iota(
        i32, (tiles, tokens), 0
    )
    token = part_of.astype(f32)
    own = (part_of >= 0) & (part_of < size)
    at_row = jnp.sum(
        jnp.where(own & (token < length), first + token + 1.0, 0.0), axis=0, keepdims=True
    ) - 1.0
    hit = lax.broadcasted_iota(i32, (rows, tokens), 0) == at_row.astype(i32)
    select = jnp.where(hit, 1.0, 0.0).astype(jnp.bfloat16)
    placed = jnp.dot(select, cap_ref[...], preferred_element_type=f32).astype(jnp.bfloat16)
    stage[...] = placed
    x[0, pl.ds(0, rs), :] = placed[:rs]
    flags = lax.dot_general(
        jnp.ones((16, tokens), jnp.bfloat16), select, (((1,), (1,)), ((), ())),
        preferred_element_type=f32,
    )
    blank = jnp.zeros((16, 128 - rs), f32)
    for p in range(groups):
        flag = jnp.concatenate([flags[:, p * rs:(p + 1) * rs], blank], axis=1).astype(jnp.bfloat16)
        if p:
            live_stage[p] = flag
        else:
            live[p] = flag

    pl.semaphore_wait(barrier, groups - 1 + 2)

    routes, flag_routes = [None], [None]
    for p in range(1, groups):
        part = pl.ds(p * rs, rs)
        to = (lax.rem(g + order[p], groups), m)
        routes.append(pltpu.make_async_remote_copy(
            src_ref=stage.at[part], dst_ref=x.at[0, part], send_sem=z_send.at[p],
            recv_sem=z_recv.at[p], device_id=to, device_id_type=MESH))
        flag_routes.append(pltpu.make_async_remote_copy(
            src_ref=live_stage.at[p], dst_ref=live.at[p], send_sem=l_send.at[p],
            recv_sem=l_recv.at[p], device_id=to, device_id_type=MESH))

    chunk_rows = rows // chunks
    chunk_slots = groups // chunks

    def ring_copy(c, h, side):
        first, count = c * chunk_rows, chunk_rows
        if h == hops:
            count = chunk_rows // 2
            first = first + (count if side else 0)
        part = pl.ds(first, count)
        source = 0 if h == 1 else 2 * (h - 1) - 1 + side
        target = n - 1 if h == hops else 2 * h - 1 + side
        return pltpu.make_async_remote_copy(
            src_ref=x.at[source, part], dst_ref=x.at[target, part],
            send_sem=r_send.at[c, h - 1, side], recv_sem=r_recv.at[c, h - 1, side],
            device_id=(g, left if side else right), device_id_type=MESH)

    def hop(c, h):
        if h == 1:
            for p in range(c * chunk_slots, (c + 1) * chunk_slots):
                if p:
                    routes[p].wait_recv()
        else:
            ring_copy(c, h - 1, 0).wait_recv()
            ring_copy(c, h - 1, 1).wait_recv()
        ring_copy(c, h, 0).start()
        ring_copy(c, h, 1).start()

    half_rows = rows // halves
    half_chunks = chunks // halves
    tile = widest(cols, (512, 256, 128))
    seen = set()

    def project(part, f):
        if f not in seen:
            seen.add(f)
            for c in weight_copies(f):
                c.wait()
        if f == n - 1:
            for c in both(part):
                ring_copy(c, hops, 0).wait_recv()
                ring_copy(c, hops, 1).wait_recv()
        span = pl.ds(part * half_rows, half_rows)

        def body(j, carry):
            at = pl.ds(pl.multiple_of(j * tile, tile), tile)
            term = jnp.dot(x[f, span, :], w[f, :, at], preferred_element_type=jnp.float32)
            if f == 0:
                acc[span, at] = term
            else:
                acc[span, at] += term
            return carry

        lax.fori_loop(0, cols // tile, body, 0)

    for p in range(1, groups):
        if p == 1:
            ring_copy(0, 1, 0).start() if chunk_slots == 1 else None
            ring_copy(0, 1, 1).start() if chunk_slots == 1 else None
        routes[p].start()
        flag_routes[p].start()

    def both(part):
        return range(part * half_chunks, (part + 1) * half_chunks)

    early = [[(c, 1)] for c in both(0)] + [[] for _ in range(hops - 1)]
    for h in range(2, hops + 1):
        for c in both(0):
            early[c + h - 1].append((c, h))
    events = early[:half_chunks - 1]
    rest = early[half_chunks - 1:]
    events.append(rest[0] + [(0, 0)])
    for i in range(max(half_chunks, hops - 1)):
        event = []
        if i < half_chunks:
            event.append((half_chunks + i, 1))
        if i + 1 < len(rest):
            event += rest[i + 1]
        events.append(event + [(0, 0)])
    for h in range(2, hops + 1):
        events.append([(c, h) for c in both(1)])

    units = [(0, f) for f in range(n)] + [(1, f) for f in range(n - 1)]
    for event in events:
        for c, h in event:
            if h == 0:
                if units:
                    project(*units.pop(0))
            elif not (c == 0 and h == 1 and chunk_slots == 1):
                hop(c, h)
    while units:
        project(*units.pop(0))

    q_copy.wait()
    for p in range(1, groups):
        flag_routes[p].wait_recv()
    for c in both(1):
        ring_copy(c, hops, 0).wait_recv()
        ring_copy(c, hops, 1).wait_recv()

    flag_row = jnp.concatenate([live[p][0:1, :rs] for p in range(groups)], axis=1)
    bias = (flag_row.astype(f32) - 1.0) * 1e30
    factor = 1.4426950408889634 / HEAD_DIM**0.5
    q_rows = q.shape[0]
    q_tile = widest(q_rows, (256, 128, 64))

    heads = head_cols // HEAD_DIM
    group_heads = widest(heads, (2, 1))
    wide = group_heads * HEAD_DIM
    done, last = pl.ds(0, half_rows), pl.ds(half_rows, half_rows)
    ones = jnp.ones((rows, HEAD_DIM), jnp.bfloat16)

    def finished(at):
        tail = acc[last, at] + jnp.dot(x[n - 1, last, :], w[n - 1, :, at], preferred_element_type=f32)
        return jnp.concatenate([acc[done, at].astype(jnp.bfloat16), tail.astype(jnp.bfloat16)], axis=0)

    def some_heads(i, carry):
        keys = finished(pl.ds(pl.multiple_of(i * wide, wide), wide))
        values = finished(pl.ds(pl.multiple_of(head_cols + i * wide, HEAD_DIM), wide))
        for j in range(group_heads):
            mine = slice(j * HEAD_DIM, (j + 1) * HEAD_DIM)
            col = pl.ds(pl.multiple_of(i * wide + j * HEAD_DIM, HEAD_DIM), HEAD_DIM)
            with_ones = jnp.concatenate([values[:, mine], ones], axis=1)
            for t in range(q_rows // q_tile):
                at = pl.ds(t * q_tile, q_tile)
                scores = lax.dot_general(
                    q[at, col], keys[:, mine], (((1,), (1,)), ((), ())), preferred_element_type=f32
                ) + bias
                top = jnp.max(scores, axis=1, keepdims=True)
                weights = jnp.exp2((scores - top) * factor).astype(jnp.bfloat16)
                total = jnp.dot(weights, with_ones, preferred_element_type=f32)
                out_ref[at, col] = (total[:, :HEAD_DIM] / total[:, HEAD_DIM:]).astype(out_ref.dtype)
        return carry

    lax.fori_loop(0, heads // group_heads, some_heads, 0)

    for p in range(1, groups):
        routes[p].wait_send()
        flag_routes[p].wait_send()
    for c in range(chunks):
        for h in range(1, hops + 1):
            for side in (0, 1):
                ring_copy(c, h, side).wait_send()


def local(captions, key_weight, value_weight, queries, tile_clip, tile_length):
    groups, n = lax.axis_size("group"), lax.axis_size("mp")
    tiles = tile_length.shape[0]
    tokens, width = captions.shape
    tile = tokens // tiles
    slots = max(2, 2 * tiles // groups)
    rs = -(-slots * tile // 16) * 16
    rows = groups * rs
    chunks, halves = min(groups, 8), 2
    head_cols = key_weight.shape[1]

    hops = n // 2
    bf = jnp.bfloat16
    vmem = pl.BlockSpec(memory_space=pltpu.VMEM)
    hbm = pl.BlockSpec(memory_space=pl.ANY)
    dma = pltpu.SemaphoreType.DMA
    return pl.pallas_call(
        functools.partial(kernel, groups, n, rs, chunks, halves),
        out_shape=jax.ShapeDtypeStruct(queries.shape, bf),
        in_specs=[vmem, vmem, vmem, hbm, hbm, hbm],
        out_specs=vmem,
        scratch_shapes=[
            pltpu.VMEM((n, rows, width), bf),
            pltpu.VMEM((n, width, 2 * head_cols), bf),
            pltpu.VMEM((rows, width), bf),
            pltpu.VMEM((groups, 16, 128), bf),
            pltpu.VMEM((groups, 16, 128), bf),
            pltpu.VMEM((rows, 2 * head_cols), jnp.float32),
            pltpu.VMEM(queries.shape, bf),
            dma((n, 2)), dma(()),
            dma((groups,)), dma((groups,)), dma((groups,)), dma((groups,)),
            dma((chunks, hops, 2)), dma((chunks, hops, 2)),
        ],
        compiler_params=pltpu.CompilerParams(
            collective_id=0, has_side_effects=True, vmem_limit_bytes=58 * 1024 * 1024
        ),
        cost_estimate=pl.CostEstimate(
            flops=4 * rows * n * width * head_cols + 4 * queries.size * rows,
            bytes_accessed=4 * key_weight.size + 4 * queries.size,
            transcendentals=queries.size * rows // HEAD_DIM,
        ),
    )(tile_clip.reshape(1, tiles), tile_length.reshape(1, tiles), captions, key_weight, value_weight, queries)


def solution(mesh):
    placed = (
        P("group", "mp"),
        P(None, "mp"),
        P(None, "mp"),
        P("group", "mp"),
        P("group", None),
        P("group"),
    )
    return jax.shard_map(
        local, mesh=mesh, in_specs=placed, out_specs=P("group", "mp"), check_vma=False
    )
```

```python
import functools

import jax
import jax.numpy as jnp
from jax import lax
from jax.experimental import pallas as pl
from jax.experimental.pallas import tpu as pltpu
from jax.sharding import PartitionSpec as P

HEAD_DIM = 128
MESH = pl.DeviceIdType.MESH


def ring_place(i, n):
    half = n // 2
    far = i // half
    return i * (1 - far) + far * (n + half - 1 - i)


def partner(g, k):
    bit = 1
    while bit <= k:
        if k & bit:
            g = g + bit - 2 * bit * lax.rem(g // bit, 2)
        bit *= 2
    return g


def widest(total, options):
    return next(o for o in options if total % o == 0)


def kernel(
    groups, n, rs, chunks, halves,
    clip_ref, length_ref, cap_ref, kw_ref, vw_ref, q_hbm, out_ref,
    x, w, stage, live_stage, live, acc, q,
    w_sem, q_sem, z_send, z_recv, l_send, l_recv, r_send, r_recv,
):
    g = lax.axis_index("group")
    m = lax.axis_index("mp")
    place = ring_place(m, n)
    right = ring_place(lax.rem(place + 1, n), n)
    left = ring_place(lax.rem(place + n - 1, n), n)
    rows, width = stage.shape
    head_cols = kw_ref.shape[1]
    cols = 2 * head_cols
    hops = n // 2

    def weight_copies(f):
        hop = (f + 1) // 2
        owner = ring_place(lax.rem(place + (n - hop if f % 2 else hop), n), n)
        part = pl.ds(pl.multiple_of(owner * width, width), width)
        return [
            pltpu.make_async_copy(kw_ref.at[part], w.at[f, :, pl.ds(0, head_cols)], w_sem.at[f, 0]),
            pltpu.make_async_copy(vw_ref.at[part], w.at[f, :, pl.ds(head_cols, head_cols)], w_sem.at[f, 1]),
        ]

    for f in range(n):
        for c in weight_copies(f):
            c.start()
    q_copy = pltpu.make_async_copy(q_hbm, q, q_sem)
    q_copy.start()

    barrier = pltpu.get_barrier_semaphore()
    for k in range(1, groups):
        pl.semaphore_signal(barrier, inc=1, device_id=(partner(g, k), m), device_id_type=MESH)
    for side in (left, right):
        pl.semaphore_signal(barrier, inc=1, device_id=(g, side), device_id_type=MESH)

    f32, i32 = jnp.float32, jnp.int32
    tokens, tiles = cap_ref.shape[0], length_ref.shape[1]
    size = tokens // tiles
    row = lax.broadcasted_iota(i32, (tiles, tiles), 0)
    column = lax.broadcasted_iota(i32, (tiles, tiles), 1)
    def upright(across):
        return jnp.sum(jnp.where(row == column, across, 0.0), axis=1, keepdims=True)

    clip_across = clip_ref[...].astype(f32)
    clip = upright(clip_across)
    length = upright(length_ref[...].astype(f32))
    rank = jnp.sum(
        jnp.where((clip == clip_across) & (column < row), 1.0, 0.0), axis=1, keepdims=True
    )
    slot = jnp.bitwise_xor(clip.astype(i32), jnp.full(clip.shape, g, i32))
    first = slot.astype(f32) * rs + rank * size
    part_of = lax.broadcasted_iota(i32, (tiles, tokens), 1) - size * lax.broadcasted_iota(
        i32, (tiles, tokens), 0
    )
    token = part_of.astype(f32)
    own = (part_of >= 0) & (part_of < size)
    at_row = jnp.sum(
        jnp.where(own & (token < length), first + token + 1.0, 0.0), axis=0, keepdims=True
    ) - 1.0
    hit = lax.broadcasted_iota(i32, (rows, tokens), 0) == at_row.astype(i32)
    select = jnp.where(hit, 1.0, 0.0).astype(jnp.bfloat16)
    placed = jnp.dot(select, cap_ref[...], preferred_element_type=f32).astype(jnp.bfloat16)
    stage[...] = placed
    x[0, pl.ds(0, rs), :] = placed[:rs]
    flags = lax.dot_general(
        jnp.ones((16, tokens), jnp.bfloat16), select, (((1,), (1,)), ((), ())),
        preferred_element_type=f32,
    )
    blank = jnp.zeros((16, 128 - rs), f32)
    for p in range(groups):
        flag = jnp.concatenate([flags[:, p * rs:(p + 1) * rs], blank], axis=1).astype(jnp.bfloat16)
        if p:
            live_stage[p] = flag
        else:
            live[p] = flag

    pl.semaphore_wait(barrier, groups - 1 + 2)

    routes, flag_routes = [None], [None]
    for p in range(1, groups):
        part = pl.ds(p * rs, rs)
        to = (partner(g, p), m)
        routes.append(pltpu.make_async_remote_copy(
            src_ref=stage.at[part], dst_ref=x.at[0, part], send_sem=z_send.at[p],
            recv_sem=z_recv.at[p], device_id=to, device_id_type=MESH))
        flag_routes.append(pltpu.make_async_remote_copy(
            src_ref=live_stage.at[p], dst_ref=live.at[p], send_sem=l_send.at[p],
            recv_sem=l_recv.at[p], device_id=to, device_id_type=MESH))

    chunk_rows = rows // chunks
    chunk_slots = groups // chunks

    def ring_copy(c, h, side):
        first, count = c * chunk_rows, chunk_rows
        if h == hops:
            count = chunk_rows // 2
            first = first + (count if side else 0)
        part = pl.ds(first, count)
        source = 0 if h == 1 else 2 * (h - 1) - 1 + side
        target = n - 1 if h == hops else 2 * h - 1 + side
        return pltpu.make_async_remote_copy(
            src_ref=x.at[source, part], dst_ref=x.at[target, part],
            send_sem=r_send.at[c, h - 1, side], recv_sem=r_recv.at[c, h - 1, side],
            device_id=(g, left if side else right), device_id_type=MESH)

    def hop(c, h):
        if h == 1:
            for p in range(c * chunk_slots, (c + 1) * chunk_slots):
                if p:
                    routes[p].wait_recv()
        else:
            ring_copy(c, h - 1, 0).wait_recv()
            ring_copy(c, h - 1, 1).wait_recv()
        ring_copy(c, h, 0).start()
        ring_copy(c, h, 1).start()

    half_rows = rows // halves
    half_chunks = chunks // halves
    tile = widest(cols, (512, 256, 128))
    seen = set()

    pieces = 2 if cols // tile > 1 else 1

    def project(part, f, piece):
        if f not in seen:
            seen.add(f)
            for c in weight_copies(f):
                c.wait()
        if f == n - 1 and piece == 0:
            for c in both(part):
                ring_copy(c, hops, 0).wait_recv()
                ring_copy(c, hops, 1).wait_recv()
        span = pl.ds(part * half_rows, half_rows)

        def body(j, carry):
            at = pl.ds(pl.multiple_of(j * tile, tile), tile)
            term = jnp.dot(x[f, span, :], w[f, :, at], preferred_element_type=jnp.float32)
            if f == 0:
                acc[span, at] = term
            else:
                acc[span, at] += term
            return carry

        steps = cols // tile
        lax.fori_loop(steps * piece // pieces, steps * (piece + 1) // pieces, body, 0)

    if chunk_slots == 1:
        hop(0, 1)
    for p in range(1, groups):
        routes[p].start()
        flag_routes[p].start()

    def both(part):
        return range(part * half_chunks, (part + 1) * half_chunks)

    events = sorted(
        ((c, h) for c in range(chunks) for h in range(1, hops + 1)),
        key=lambda e: (e[0] + (1.5 if e[0] < half_chunks else 2.5) * (e[1] - 1), e[1]),
    )
    units = [(0, f, i) for f in range(n) for i in range(pieces)]
    units += [(1, f, i) for f in range(n - 1) for i in range(pieces)]
    begun = set()

    def ready(part, f, piece):
        need = hops if f == n - 1 else (f + 1) // 2 + 1
        return all((c, need) in begun for c in both(part))

    for c, h in events:
        if not (c == 0 and h == 1 and chunk_slots == 1):
            hop(c, h)
        begun.add((c, h))
        if units and ready(*units[0]):
            project(*units.pop(0))
    while units:
        project(*units.pop(0))

    q_copy.wait()
    for p in range(1, groups):
        flag_routes[p].wait_recv()
    for c in both(1):
        ring_copy(c, hops, 0).wait_recv()
        ring_copy(c, hops, 1).wait_recv()

    flag_row = jnp.concatenate([live[p][0:1, :rs] for p in range(groups)], axis=1)
    bias = (flag_row.astype(f32) - 1.0) * 1e30
    factor = 1.4426950408889634 / HEAD_DIM**0.5
    q_rows = q.shape[0]
    q_tile = widest(q_rows, (256, 128, 64))

    heads = head_cols // HEAD_DIM
    group_heads = widest(heads, (2, 1))
    wide = group_heads * HEAD_DIM
    done, last = pl.ds(0, half_rows), pl.ds(half_rows, half_rows)
    ones = jnp.ones((rows, HEAD_DIM), jnp.bfloat16)

    def finished(at):
        tail = acc[last, at] + jnp.dot(x[n - 1, last, :], w[n - 1, :, at], preferred_element_type=f32)
        return jnp.concatenate([acc[done, at].astype(jnp.bfloat16), tail.astype(jnp.bfloat16)], axis=0)

    def some_heads(i, carry):
        keys = finished(pl.ds(pl.multiple_of(i * wide, wide), wide))
        values = finished(pl.ds(pl.multiple_of(head_cols + i * wide, HEAD_DIM), wide))
        for j in range(group_heads):
            mine = slice(j * HEAD_DIM, (j + 1) * HEAD_DIM)
            col = pl.ds(pl.multiple_of(i * wide + j * HEAD_DIM, HEAD_DIM), HEAD_DIM)
            with_ones = jnp.concatenate([values[:, mine], ones], axis=1)
            for t in range(q_rows // q_tile):
                at = pl.ds(t * q_tile, q_tile)
                scores = lax.dot_general(
                    q[at, col], keys[:, mine], (((1,), (1,)), ((), ())), preferred_element_type=f32
                ) + bias
                top = jnp.max(scores, axis=1, keepdims=True)
                weights = jnp.exp2((scores - top) * factor).astype(jnp.bfloat16)
                total = jnp.dot(weights, with_ones, preferred_element_type=f32)
                out_ref[at, col] = (total[:, :HEAD_DIM] / total[:, HEAD_DIM:]).astype(out_ref.dtype)
        return carry

    lax.fori_loop(0, heads // group_heads, some_heads, 0)

    for p in range(1, groups):
        routes[p].wait_send()
        flag_routes[p].wait_send()
    for c in range(chunks):
        for h in range(1, hops + 1):
            for side in (0, 1):
                ring_copy(c, h, side).wait_send()


def local(captions, key_weight, value_weight, queries, tile_clip, tile_length):
    groups, n = lax.axis_size("group"), lax.axis_size("mp")
    tiles = tile_length.shape[0]
    tokens, width = captions.shape
    tile = tokens // tiles
    slots = max(2, 2 * tiles // groups)
    rs = -(-slots * tile // 16) * 16
    rows = groups * rs
    chunks, halves = min(groups, 8), 2
    head_cols = key_weight.shape[1]

    hops = n // 2
    bf = jnp.bfloat16
    vmem = pl.BlockSpec(memory_space=pltpu.VMEM)
    hbm = pl.BlockSpec(memory_space=pl.ANY)
    dma = pltpu.SemaphoreType.DMA
    return pl.pallas_call(
        functools.partial(kernel, groups, n, rs, chunks, halves),
        out_shape=jax.ShapeDtypeStruct(queries.shape, bf),
        in_specs=[vmem, vmem, vmem, hbm, hbm, hbm],
        out_specs=vmem,
        scratch_shapes=[
            pltpu.VMEM((n, rows, width), bf),
            pltpu.VMEM((n, width, 2 * head_cols), bf),
            pltpu.VMEM((rows, width), bf),
            pltpu.VMEM((groups, 16, 128), bf),
            pltpu.VMEM((groups, 16, 128), bf),
            pltpu.VMEM((rows, 2 * head_cols), jnp.float32),
            pltpu.VMEM(queries.shape, bf),
            dma((n, 2)), dma(()),
            dma((groups,)), dma((groups,)), dma((groups,)), dma((groups,)),
            dma((chunks, hops, 2)), dma((chunks, hops, 2)),
        ],
        compiler_params=pltpu.CompilerParams(
            collective_id=0, has_side_effects=True, vmem_limit_bytes=58 * 1024 * 1024
        ),
        cost_estimate=pl.CostEstimate(
            flops=4 * rows * n * width * head_cols + 4 * queries.size * rows,
            bytes_accessed=4 * key_weight.size + 4 * queries.size,
            transcendentals=queries.size * rows // HEAD_DIM,
        ),
    )(tile_clip.reshape(1, tiles), tile_length.reshape(1, tiles), captions, key_weight, value_weight, queries)


def solution(mesh):
    placed = (
        P("group", "mp"),
        P(None, "mp"),
        P(None, "mp"),
        P("group", "mp"),
        P("group", None),
        P("group"),
    )
    return jax.shard_map(
        local, mesh=mesh, in_specs=placed, out_specs=P("group", "mp"), check_vma=False
    )
```

```python
import functools

import jax
import jax.numpy as jnp
from jax import lax
from jax.experimental import pallas as pl
from jax.experimental.pallas import tpu as pltpu
from jax.sharding import PartitionSpec as P

HEAD_DIM = 128
MESH = pl.DeviceIdType.MESH


def ring_place(i, n):
    half = n // 2
    far = i // half
    return i * (1 - far) + far * (n + half - 1 - i)


def partner(g, k):
    bit = 1
    while bit <= k:
        if k & bit:
            g = g + bit - 2 * bit * lax.rem(g // bit, 2)
        bit *= 2
    return g


def offsets_of(groups):
    half = groups // 2
    near, far = list(range(1, half)), list(range(half, groups))
    order = [0]
    while near or far:
        order += near[:1] + far[:1]
        near, far = near[1:], far[1:]
    return order


def widest(total, options):
    return next(o for o in options if total % o == 0)


def kernel(
    groups, n, rs, chunks, halves,
    clip_ref, length_ref, cap_ref, kw_ref, vw_ref, q_hbm, out_ref,
    x, w, stage, live_stage, live, acc, q,
    w_sem, q_sem, z_send, z_recv, l_send, l_recv, r_send, r_recv,
):
    g = lax.axis_index("group")
    m = lax.axis_index("mp")
    place = ring_place(m, n)
    right = ring_place(lax.rem(place + 1, n), n)
    left = ring_place(lax.rem(place + n - 1, n), n)
    rows, width = stage.shape
    head_cols = kw_ref.shape[1]
    cols = 2 * head_cols
    hops = n // 2
    order = offsets_of(groups)

    def weight_copies(f):
        hop = (f + 1) // 2
        owner = ring_place(lax.rem(place + (n - hop if f % 2 else hop), n), n)
        part = pl.ds(pl.multiple_of(owner * width, width), width)
        return [
            pltpu.make_async_copy(kw_ref.at[part], w.at[f, :, pl.ds(0, head_cols)], w_sem.at[f, 0]),
            pltpu.make_async_copy(vw_ref.at[part], w.at[f, :, pl.ds(head_cols, head_cols)], w_sem.at[f, 1]),
        ]

    for f in range(n):
        for c in weight_copies(f):
            c.start()
    q_copy = pltpu.make_async_copy(q_hbm, q, q_sem)
    q_copy.start()

    barrier = pltpu.get_barrier_semaphore()
    for k in range(1, groups):
        pl.semaphore_signal(barrier, inc=1, device_id=(partner(g, k), m), device_id_type=MESH)
    for side in (left, right):
        pl.semaphore_signal(barrier, inc=1, device_id=(g, side), device_id_type=MESH)

    f32, i32 = jnp.float32, jnp.int32
    tokens, tiles = cap_ref.shape[0], length_ref.shape[1]
    size = tokens // tiles
    row = lax.broadcasted_iota(i32, (tiles, tiles), 0)
    column = lax.broadcasted_iota(i32, (tiles, tiles), 1)
    def upright(across):
        return jnp.sum(jnp.where(row == column, across, 0.0), axis=1, keepdims=True)

    clip_across = clip_ref[...].astype(f32)
    clip = upright(clip_across)
    length = upright(length_ref[...].astype(f32))
    rank = jnp.sum(
        jnp.where((clip == clip_across) & (column < row), 1.0, 0.0), axis=1, keepdims=True
    )
    off = jnp.bitwise_xor(clip.astype(i32), jnp.full(clip.shape, g, i32))
    far = jnp.minimum(2 * off + 2 - groups, groups - 1)
    slot = jnp.where(off == 0, 0, jnp.where(off < groups // 2, 2 * off - 1, far))
    first = slot.astype(f32) * rs + rank * size
    part_of = lax.broadcasted_iota(i32, (tiles, tokens), 1) - size * lax.broadcasted_iota(
        i32, (tiles, tokens), 0
    )
    token = part_of.astype(f32)
    own = (part_of >= 0) & (part_of < size)
    at_row = jnp.sum(
        jnp.where(own & (token < length), first + token + 1.0, 0.0), axis=0, keepdims=True
    ) - 1.0
    hit = lax.broadcasted_iota(i32, (rows, tokens), 0) == at_row.astype(i32)
    select = jnp.where(hit, 1.0, 0.0).astype(jnp.bfloat16)
    placed = jnp.dot(select, cap_ref[...], preferred_element_type=f32).astype(jnp.bfloat16)
    stage[...] = placed
    x[0, pl.ds(0, rs), :] = placed[:rs]
    flags = lax.dot_general(
        jnp.ones((16, tokens), jnp.bfloat16), select, (((1,), (1,)), ((), ())),
        preferred_element_type=f32,
    )
    blank = jnp.zeros((16, 128 - rs), f32)
    for p in range(groups):
        flag = jnp.concatenate([flags[:, p * rs:(p + 1) * rs], blank], axis=1).astype(jnp.bfloat16)
        if p:
            live_stage[p] = flag
        else:
            live[p] = flag

    pl.semaphore_wait(barrier, groups - 1 + 2)

    routes, flag_routes = [None], [None]
    for p in range(1, groups):
        part = pl.ds(p * rs, rs)
        to = (partner(g, order[p]), m)
        routes.append(pltpu.make_async_remote_copy(
            src_ref=stage.at[part], dst_ref=x.at[0, part], send_sem=z_send.at[p],
            recv_sem=z_recv.at[p], device_id=to, device_id_type=MESH))
        flag_routes.append(pltpu.make_async_remote_copy(
            src_ref=live_stage.at[p], dst_ref=live.at[p], send_sem=l_send.at[p],
            recv_sem=l_recv.at[p], device_id=to, device_id_type=MESH))

    chunk_rows = rows // chunks
    chunk_slots = groups // chunks

    def ring_copy(c, h, side):
        first, count = c * chunk_rows, chunk_rows
        if h == hops:
            count = chunk_rows // 2
            first = first + (count if side else 0)
        part = pl.ds(first, count)
        source = 0 if h == 1 else 2 * (h - 1) - 1 + side
        target = n - 1 if h == hops else 2 * h - 1 + side
        return pltpu.make_async_remote_copy(
            src_ref=x.at[source, part], dst_ref=x.at[target, part],
            send_sem=r_send.at[c, h - 1, side], recv_sem=r_recv.at[c, h - 1, side],
            device_id=(g, left if side else right), device_id_type=MESH)

    def hop(c, h):
        if h == 1:
            for p in range(c * chunk_slots, (c + 1) * chunk_slots):
                if p:
                    routes[p].wait_recv()
        else:
            ring_copy(c, h - 1, 0).wait_recv()
            ring_copy(c, h - 1, 1).wait_recv()
        ring_copy(c, h, 0).start()
        ring_copy(c, h, 1).start()

    half_rows = rows // halves
    half_chunks = chunks // halves
    tile = widest(cols, (512, 256, 128))
    seen = set()

    pieces = 2 if cols // tile > 1 else 1

    def project(part, f, piece):
        if f not in seen:
            seen.add(f)
            for c in weight_copies(f):
                c.wait()
        if f == n - 1 and piece == 0:
            for c in both(part):
                ring_copy(c, hops, 0).wait_recv()
                ring_copy(c, hops, 1).wait_recv()
        span = pl.ds(part * half_rows, half_rows)

        def body(j, carry):
            at = pl.ds(pl.multiple_of(j * tile, tile), tile)
            term = jnp.dot(x[f, span, :], w[f, :, at], preferred_element_type=jnp.float32)
            if f == 0:
                acc[span, at] = term
            else:
                acc[span, at] += term
            return carry

        steps = cols // tile
        lax.fori_loop(steps * piece // pieces, steps * (piece + 1) // pieces, body, 0)

    if chunk_slots == 1:
        hop(0, 1)
    for p in range(1, groups):
        routes[p].start()
        flag_routes[p].start()

    def both(part):
        return range(part * half_chunks, (part + 1) * half_chunks)

    events = sorted(
        ((c, h) for c in range(chunks) for h in range(1, hops + 1)),
        key=lambda e: (e[0] + (1.5 if e[0] < half_chunks else 2.5) * (e[1] - 1), e[1]),
    )
    units = [(0, f, i) for f in range(n) for i in range(pieces)]
    units += [(1, f, i) for f in range(n - 1) for i in range(pieces)]
    begun = set()

    def ready(part, f, piece):
        need = hops if f == n - 1 else (f + 1) // 2 + 1
        return all((c, need) in begun for c in both(part))

    for c, h in events:
        if not (c == 0 and h == 1 and chunk_slots == 1):
            hop(c, h)
        begun.add((c, h))
        if units and ready(*units[0]):
            project(*units.pop(0))
    while units:
        project(*units.pop(0))

    q_copy.wait()
    for p in range(1, groups):
        flag_routes[p].wait_recv()
    for c in both(1):
        ring_copy(c, hops, 0).wait_recv()
        ring_copy(c, hops, 1).wait_recv()

    flag_row = jnp.concatenate([live[p][0:1, :rs] for p in range(groups)], axis=1)
    bias = (flag_row.astype(f32) - 1.0) * 1e30
    factor = 1.4426950408889634 / HEAD_DIM**0.5
    q_rows = q.shape[0]
    q_tile = widest(q_rows, (256, 128, 64))

    heads = head_cols // HEAD_DIM
    group_heads = widest(heads, (2, 1))
    wide = group_heads * HEAD_DIM
    done, last = pl.ds(0, half_rows), pl.ds(half_rows, half_rows)
    ones = jnp.ones((rows, HEAD_DIM), jnp.bfloat16)

    def finished(at):
        tail = acc[last, at] + jnp.dot(x[n - 1, last, :], w[n - 1, :, at], preferred_element_type=f32)
        return jnp.concatenate([acc[done, at].astype(jnp.bfloat16), tail.astype(jnp.bfloat16)], axis=0)

    def some_heads(i, carry):
        keys = finished(pl.ds(pl.multiple_of(i * wide, wide), wide))
        values = finished(pl.ds(pl.multiple_of(head_cols + i * wide, HEAD_DIM), wide))
        for j in range(group_heads):
            mine = slice(j * HEAD_DIM, (j + 1) * HEAD_DIM)
            col = pl.ds(pl.multiple_of(i * wide + j * HEAD_DIM, HEAD_DIM), HEAD_DIM)
            with_ones = jnp.concatenate([values[:, mine], ones], axis=1)
            for t in range(q_rows // q_tile):
                at = pl.ds(t * q_tile, q_tile)
                scores = lax.dot_general(
                    q[at, col], keys[:, mine], (((1,), (1,)), ((), ())), preferred_element_type=f32
                ) + bias
                top = jnp.max(scores, axis=1, keepdims=True)
                weights = jnp.exp2((scores - top) * factor).astype(jnp.bfloat16)
                total = jnp.dot(weights, with_ones, preferred_element_type=f32)
                out_ref[at, col] = (total[:, :HEAD_DIM] / total[:, HEAD_DIM:]).astype(out_ref.dtype)
        return carry

    lax.fori_loop(0, heads // group_heads, some_heads, 0)

    for p in range(1, groups):
        routes[p].wait_send()
        flag_routes[p].wait_send()
    for c in range(chunks):
        for h in range(1, hops + 1):
            for side in (0, 1):
                ring_copy(c, h, side).wait_send()


def local(captions, key_weight, value_weight, queries, tile_clip, tile_length):
    groups, n = lax.axis_size("group"), lax.axis_size("mp")
    tiles = tile_length.shape[0]
    tokens, width = captions.shape
    tile = tokens // tiles
    slots = max(2, 2 * tiles // groups)
    rs = -(-slots * tile // 16) * 16
    rows = groups * rs
    chunks, halves = min(groups, 8), 2
    head_cols = key_weight.shape[1]

    hops = n // 2
    bf = jnp.bfloat16
    vmem = pl.BlockSpec(memory_space=pltpu.VMEM)
    hbm = pl.BlockSpec(memory_space=pl.ANY)
    dma = pltpu.SemaphoreType.DMA
    return pl.pallas_call(
        functools.partial(kernel, groups, n, rs, chunks, halves),
        out_shape=jax.ShapeDtypeStruct(queries.shape, bf),
        in_specs=[vmem, vmem, vmem, hbm, hbm, hbm],
        out_specs=vmem,
        scratch_shapes=[
            pltpu.VMEM((n, rows, width), bf),
            pltpu.VMEM((n, width, 2 * head_cols), bf),
            pltpu.VMEM((rows, width), bf),
            pltpu.VMEM((groups, 16, 128), bf),
            pltpu.VMEM((groups, 16, 128), bf),
            pltpu.VMEM((rows, 2 * head_cols), jnp.float32),
            pltpu.VMEM(queries.shape, bf),
            dma((n, 2)), dma(()),
            dma((groups,)), dma((groups,)), dma((groups,)), dma((groups,)),
            dma((chunks, hops, 2)), dma((chunks, hops, 2)),
        ],
        compiler_params=pltpu.CompilerParams(
            collective_id=0, has_side_effects=True, vmem_limit_bytes=58 * 1024 * 1024
        ),
        cost_estimate=pl.CostEstimate(
            flops=4 * rows * n * width * head_cols + 4 * queries.size * rows,
            bytes_accessed=4 * key_weight.size + 4 * queries.size,
            transcendentals=queries.size * rows // HEAD_DIM,
        ),
    )(tile_clip.reshape(1, tiles), tile_length.reshape(1, tiles), captions, key_weight, value_weight, queries)


def solution(mesh):
    placed = (
        P("group", "mp"),
        P(None, "mp"),
        P(None, "mp"),
        P("group", "mp"),
        P("group", None),
        P("group"),
    )
    return jax.shard_map(
        local, mesh=mesh, in_specs=placed, out_specs=P("group", "mp"), check_vma=False
    )
```

```python
import functools

import jax
import jax.numpy as jnp
from jax import lax
from jax.experimental import pallas as pl
from jax.experimental.pallas import tpu as pltpu
from jax.sharding import PartitionSpec as P

HEAD_DIM = 128
MESH = pl.DeviceIdType.MESH


def ring_place(i, n):
    half = n // 2
    far = i // half
    return i * (1 - far) + far * (n + half - 1 - i)


def partner(g, k):
    bit = 1
    while bit <= k:
        if k & bit:
            g = g + bit - 2 * bit * lax.rem(g // bit, 2)
        bit *= 2
    return g


def offsets_of(groups):
    half = groups // 2
    near, far = list(range(1, half)), list(range(half, groups))
    order = [0]
    while near or far:
        order += near[:1] + far[:1]
        near, far = near[1:], far[1:]
    return order


def widest(total, options):
    return next(o for o in options if total % o == 0)


def kernel(
    groups, n, rs, chunks, halves,
    clip_ref, length_ref, cap_ref, kw_ref, vw_ref, q_hbm, out_ref,
    x, w, stage, live_stage, live, acc, q, early_sum, early_top,
    w_sem, q_sem, z_send, z_recv, l_send, l_recv, r_send, r_recv,
):
    g = lax.axis_index("group")
    m = lax.axis_index("mp")
    place = ring_place(m, n)
    right = ring_place(lax.rem(place + 1, n), n)
    left = ring_place(lax.rem(place + n - 1, n), n)
    rows, width = stage.shape
    head_cols = kw_ref.shape[1]
    cols = 2 * head_cols
    hops = n // 2
    order = offsets_of(groups)

    def weight_copies(f):
        hop = (f + 1) // 2
        owner = ring_place(lax.rem(place + (n - hop if f % 2 else hop), n), n)
        part = pl.ds(pl.multiple_of(owner * width, width), width)
        return [
            pltpu.make_async_copy(kw_ref.at[part], w.at[f, :, pl.ds(0, head_cols)], w_sem.at[f, 0]),
            pltpu.make_async_copy(vw_ref.at[part], w.at[f, :, pl.ds(head_cols, head_cols)], w_sem.at[f, 1]),
        ]

    for f in range(n):
        for c in weight_copies(f):
            c.start()
    q_copy = pltpu.make_async_copy(q_hbm, q, q_sem)
    q_copy.start()

    barrier = pltpu.get_barrier_semaphore()
    for k in range(1, groups):
        pl.semaphore_signal(barrier, inc=1, device_id=(partner(g, k), m), device_id_type=MESH)
    for side in (left, right):
        pl.semaphore_signal(barrier, inc=1, device_id=(g, side), device_id_type=MESH)

    f32, i32 = jnp.float32, jnp.int32
    tokens, tiles = cap_ref.shape[0], length_ref.shape[1]
    size = tokens // tiles
    row = lax.broadcasted_iota(i32, (tiles, tiles), 0)
    column = lax.broadcasted_iota(i32, (tiles, tiles), 1)
    def upright(across):
        return jnp.sum(jnp.where(row == column, across, 0.0), axis=1, keepdims=True)

    clip_across = clip_ref[...].astype(f32)
    clip = upright(clip_across)
    length = upright(length_ref[...].astype(f32))
    rank = jnp.sum(
        jnp.where((clip == clip_across) & (column < row), 1.0, 0.0), axis=1, keepdims=True
    )
    off = jnp.bitwise_xor(clip.astype(i32), jnp.full(clip.shape, g, i32))
    far = jnp.minimum(2 * off + 2 - groups, groups - 1)
    slot = jnp.where(off == 0, 0, jnp.where(off < groups // 2, 2 * off - 1, far))
    first = slot.astype(f32) * rs + rank * size
    part_of = lax.broadcasted_iota(i32, (tiles, tokens), 1) - size * lax.broadcasted_iota(
        i32, (tiles, tokens), 0
    )
    token = part_of.astype(f32)
    own = (part_of >= 0) & (part_of < size)
    at_row = jnp.sum(
        jnp.where(own & (token < length), first + token + 1.0, 0.0), axis=0, keepdims=True
    ) - 1.0
    hit = lax.broadcasted_iota(i32, (rows, tokens), 0) == at_row.astype(i32)
    select = jnp.where(hit, 1.0, 0.0).astype(jnp.bfloat16)
    placed = jnp.dot(select, cap_ref[...], preferred_element_type=f32).astype(jnp.bfloat16)
    stage[...] = placed
    x[0, pl.ds(0, rs), :] = placed[:rs]
    flags = lax.dot_general(
        jnp.ones((16, tokens), jnp.bfloat16), select, (((1,), (1,)), ((), ())),
        preferred_element_type=f32,
    )
    blank = jnp.zeros((16, 128 - rs), f32)
    for p in range(groups):
        flag = jnp.concatenate([flags[:, p * rs:(p + 1) * rs], blank], axis=1).astype(jnp.bfloat16)
        if p:
            live_stage[p] = flag
        else:
            live[p] = flag

    pl.semaphore_wait(barrier, groups - 1 + 2)

    routes, flag_routes = [None], [None]
    for p in range(1, groups):
        part = pl.ds(p * rs, rs)
        to = (partner(g, order[p]), m)
        routes.append(pltpu.make_async_remote_copy(
            src_ref=stage.at[part], dst_ref=x.at[0, part], send_sem=z_send.at[p],
            recv_sem=z_recv.at[p], device_id=to, device_id_type=MESH))
        flag_routes.append(pltpu.make_async_remote_copy(
            src_ref=live_stage.at[p], dst_ref=live.at[p], send_sem=l_send.at[p],
            recv_sem=l_recv.at[p], device_id=to, device_id_type=MESH))

    chunk_rows = rows // chunks
    chunk_slots = groups // chunks

    def ring_copy(c, h, side):
        first, count = c * chunk_rows, chunk_rows
        if h == hops:
            count = chunk_rows // 2
            first = first + (count if side else 0)
        part = pl.ds(first, count)
        source = 0 if h == 1 else 2 * (h - 1) - 1 + side
        target = n - 1 if h == hops else 2 * h - 1 + side
        return pltpu.make_async_remote_copy(
            src_ref=x.at[source, part], dst_ref=x.at[target, part],
            send_sem=r_send.at[c, h - 1, side], recv_sem=r_recv.at[c, h - 1, side],
            device_id=(g, left if side else right), device_id_type=MESH)

    def hop(c, h):
        if h == 1:
            for p in range(c * chunk_slots, (c + 1) * chunk_slots):
                if p:
                    routes[p].wait_recv()
        else:
            ring_copy(c, h - 1, 0).wait_recv()
            ring_copy(c, h - 1, 1).wait_recv()
        ring_copy(c, h, 0).start()
        ring_copy(c, h, 1).start()

    half_rows = rows // halves
    half_chunks = chunks // halves
    tile = widest(cols, (512, 256, 128))
    seen = set()

    pieces = 2 if cols // tile > 1 else 1

    def project(part, f, piece):
        if f not in seen:
            seen.add(f)
            for c in weight_copies(f):
                c.wait()
        if f == n - 1 and piece == 0:
            for c in both(part):
                ring_copy(c, hops, 0).wait_recv()
                ring_copy(c, hops, 1).wait_recv()
        span = pl.ds(part * half_rows, half_rows)

        def body(j, carry):
            at = pl.ds(pl.multiple_of(j * tile, tile), tile)
            term = jnp.dot(x[f, span, :], w[f, :, at], preferred_element_type=jnp.float32)
            if f == 0:
                acc[span, at] = term
            else:
                acc[span, at] += term
            return carry

        steps = cols // tile
        lax.fori_loop(steps * piece // pieces, steps * (piece + 1) // pieces, body, 0)

    if chunk_slots == 1:
        hop(0, 1)
    for p in range(1, groups):
        routes[p].start()
        flag_routes[p].start()

    def both(part):
        return range(part * half_chunks, (part + 1) * half_chunks)

    factor = 1.4426950408889634 / HEAD_DIM**0.5
    q_rows = q.shape[0]
    q_tile = widest(q_rows, (256, 128, 64))
    heads = head_cols // HEAD_DIM
    group_heads = widest(heads, (2, 1))
    wide = group_heads * HEAD_DIM
    halves_of = pl.ds(0, half_rows), pl.ds(half_rows, half_rows)
    ones = jnp.ones((half_rows, HEAD_DIM), jnp.bfloat16)
    part_slots = groups // halves

    def bias_of(part):
        slots_of = range(part * part_slots, (part + 1) * part_slots)
        row = jnp.concatenate([live[p][0:1, :rs] for p in slots_of], axis=1)
        return (row.astype(f32) - 1.0) * 1e30

    def columns_of(i):
        return (pl.ds(pl.multiple_of(i * wide, HEAD_DIM), wide),
                pl.ds(pl.multiple_of(head_cols + i * wide, HEAD_DIM), wide))

    def each_head(i, keys, values, use):
        for j in range(group_heads):
            mine = slice(j * HEAD_DIM, (j + 1) * HEAD_DIM)
            col = pl.ds(pl.multiple_of(i * wide + j * HEAD_DIM, HEAD_DIM), HEAD_DIM)
            double = pl.ds(pl.multiple_of(2 * i * wide + 2 * j * HEAD_DIM, HEAD_DIM), 2 * HEAD_DIM)
            with_ones = jnp.concatenate([values[:, mine], ones], axis=1)
            for t in range(q_rows // q_tile):
                at = pl.ds(t * q_tile, q_tile)
                scores = lax.dot_general(
                    q[at, col], keys[:, mine], (((1,), (1,)), ((), ())), preferred_element_type=f32
                )
                use(scores, with_ones, at, col, double)

    def weigh(scores, top, with_ones):
        weights = jnp.exp2((scores - top) * factor).astype(jnp.bfloat16)
        return jnp.dot(weights, with_ones, preferred_element_type=f32)

    def attend_early(begin, end):
        if begin == 0:
            q_copy.wait()
            for p in range(1, part_slots):
                flag_routes[p].wait_recv()
        bias = bias_of(0)

        def use(scores, with_ones, at, col, double):
            scores = scores + bias
            top = jnp.max(scores, axis=1, keepdims=True)
            early_top[at, col] = jnp.broadcast_to(top, (q_tile, HEAD_DIM))
            early_sum[at, double] = weigh(scores, top, with_ones)

        def body(i, carry):
            keys, values = (acc[halves_of[0], c].astype(jnp.bfloat16) for c in columns_of(i))
            each_head(i, keys, values, use)
            return carry

        lax.fori_loop(begin, end, body, 0)

    def attend_late():
        bias = bias_of(1)

        def use(scores, with_ones, at, col, double):
            scores = scores + bias
            before = early_top[at, col]
            top = jnp.maximum(jnp.max(scores, axis=1, keepdims=True), before)
            total = weigh(scores, top[:, :1], with_ones)
            keep = jnp.exp2((before - top) * factor)
            earlier = early_sum[at, double]
            above = total[:, :HEAD_DIM] + keep * earlier[:, :HEAD_DIM]
            below = total[:, HEAD_DIM:] + keep * earlier[:, HEAD_DIM:]
            out_ref[at, col] = (above / below).astype(out_ref.dtype)

        def body(i, carry):
            keys, values = (
                (acc[halves_of[1], c] + jnp.dot(
                    x[n - 1, halves_of[1], :], w[n - 1, :, c], preferred_element_type=f32
                )).astype(jnp.bfloat16)
                for c in columns_of(i)
            )
            each_head(i, keys, values, use)
            return carry

        lax.fori_loop(0, heads // group_heads, body, 0)

    events = sorted(
        ((c, h) for c in range(chunks) for h in range(1, hops + 1)),
        key=lambda e: (e[0] + (1.5 if e[0] < half_chunks else half_chunks + 0.5) * (e[1] - 1), e[1]),
    )
    units = [(0, f, i) for f in range(n) for i in range(pieces)]
    units += [(1, f, i) for f in range(n - 1) for i in range(pieces)]
    begun = set()

    def ready(part, f, piece):
        need = hops if f == n - 1 else (f + 1) // 2 + 1
        return all((c, need) in begun for c in both(part))

    loops = heads // group_heads
    for c, h in events:
        if (c, h) == (chunks - 1, hops):
            while units and units[0][0] == 0:
                project(*units.pop(0))
            attend_early(0, loops // 2)
        if not (c == 0 and h == 1 and chunk_slots == 1):
            hop(c, h)
        begun.add((c, h))
        later = c >= half_chunks
        for _ in range(1 if not later or c == half_chunks else 2):
            if units and not (later and h > 1) and ready(*units[0]):
                project(*units.pop(0))
    attend_early(loops // 2, loops)
    while units:
        project(*units.pop(0))

    for p in range(part_slots, groups):
        flag_routes[p].wait_recv()
    for c in both(1):
        ring_copy(c, hops, 0).wait_recv()
        ring_copy(c, hops, 1).wait_recv()
    attend_late()

    for p in range(1, groups):
        routes[p].wait_send()
        flag_routes[p].wait_send()
    for c in range(chunks):
        for h in range(1, hops + 1):
            for side in (0, 1):
                ring_copy(c, h, side).wait_send()


def local(captions, key_weight, value_weight, queries, tile_clip, tile_length):
    groups, n = lax.axis_size("group"), lax.axis_size("mp")
    tiles = tile_length.shape[0]
    tokens, width = captions.shape
    tile = tokens // tiles
    slots = max(2, 2 * tiles // groups)
    rs = -(-slots * tile // 16) * 16
    rows = groups * rs
    chunks, halves = min(groups, 8), 2
    head_cols = key_weight.shape[1]

    hops = n // 2
    bf = jnp.bfloat16
    vmem = pl.BlockSpec(memory_space=pltpu.VMEM)
    hbm = pl.BlockSpec(memory_space=pl.ANY)
    dma = pltpu.SemaphoreType.DMA
    return pl.pallas_call(
        functools.partial(kernel, groups, n, rs, chunks, halves),
        out_shape=jax.ShapeDtypeStruct(queries.shape, bf),
        in_specs=[vmem, vmem, vmem, hbm, hbm, hbm],
        out_specs=vmem,
        scratch_shapes=[
            pltpu.VMEM((n, rows, width), bf),
            pltpu.VMEM((n, width, 2 * head_cols), bf),
            pltpu.VMEM((rows, width), bf),
            pltpu.VMEM((groups, 16, 128), bf),
            pltpu.VMEM((groups, 16, 128), bf),
            pltpu.VMEM((rows, 2 * head_cols), jnp.float32),
            pltpu.VMEM(queries.shape, bf),
            pltpu.VMEM((queries.shape[0], 2 * head_cols), jnp.float32),
            pltpu.VMEM(queries.shape, jnp.float32),
            dma((n, 2)), dma(()),
            dma((groups,)), dma((groups,)), dma((groups,)), dma((groups,)),
            dma((chunks, hops, 2)), dma((chunks, hops, 2)),
        ],
        compiler_params=pltpu.CompilerParams(
            collective_id=0, has_side_effects=True, vmem_limit_bytes=58 * 1024 * 1024
        ),
        cost_estimate=pl.CostEstimate(
            flops=4 * rows * n * width * head_cols + 4 * queries.size * rows,
            bytes_accessed=4 * key_weight.size + 4 * queries.size,
            transcendentals=queries.size * rows // HEAD_DIM,
        ),
    )(tile_clip.reshape(1, tiles), tile_length.reshape(1, tiles), captions, key_weight, value_weight, queries)


def solution(mesh):
    placed = (
        P("group", "mp"),
        P(None, "mp"),
        P(None, "mp"),
        P("group", "mp"),
        P("group", None),
        P("group"),
    )
    return jax.shard_map(
        local, mesh=mesh, in_specs=placed, out_specs=P("group", "mp"), check_vma=False
    )
```

```python
import functools

import jax
import jax.numpy as jnp
from jax import lax
from jax.experimental import pallas as pl
from jax.experimental.pallas import tpu as pltpu
from jax.sharding import PartitionSpec as P

HEAD_DIM = 128
MESH = pl.DeviceIdType.MESH


def ring_place(i, n):
    half = n // 2
    far = i // half
    return i * (1 - far) + far * (n + half - 1 - i)


def offsets_of(groups):
    order = [0]
    for k in range(1, groups // 2 + 1):
        order.append(k)
        if groups - k != k:
            order.append(groups - k)
    return order


def widest(total, options):
    return next(o for o in options if total % o == 0)


def kernel(
    groups, n, rs, chunks, halves,
    clip_ref, length_ref, cap_ref, kw_ref, vw_ref, q_hbm, out_ref,
    x, w, stage, live_stage, live, acc, q,
    w_sem, q_sem, z_send, z_recv, l_send, l_recv, r_send, r_recv,
):
    g = lax.axis_index("group")
    m = lax.axis_index("mp")
    place = ring_place(m, n)
    right = ring_place(lax.rem(place + 1, n), n)
    left = ring_place(lax.rem(place + n - 1, n), n)
    rows, width = stage.shape
    head_cols = kw_ref.shape[1]
    cols = 2 * head_cols
    hops = n // 2
    order = offsets_of(groups)

    def weight_copies(f):
        hop = (f + 1) // 2
        owner = ring_place(lax.rem(place + (n - hop if f % 2 else hop), n), n)
        part = pl.ds(pl.multiple_of(owner * width, width), width)
        return [
            pltpu.make_async_copy(kw_ref.at[part], w.at[pl.ds(f * width, width), pl.ds(0, head_cols)], w_sem.at[f, 0]),
            pltpu.make_async_copy(vw_ref.at[part], w.at[pl.ds(f * width, width), pl.ds(head_cols, head_cols)], w_sem.at[f, 1]),
        ]

    for f in range(n):
        for c in weight_copies(f):
            c.start()
    q_copy = pltpu.make_async_copy(q_hbm, q, q_sem)
    q_copy.start()

    barrier = pltpu.get_barrier_semaphore()
    for k in order[1:]:
        pl.semaphore_signal(barrier, inc=1, device_id=(lax.rem(g + k, groups), m), device_id_type=MESH)
    for side in (left, right):
        pl.semaphore_signal(barrier, inc=1, device_id=(g, side), device_id_type=MESH)

    f32, i32 = jnp.float32, jnp.int32
    tokens, tiles = cap_ref.shape[0], length_ref.shape[1]
    size = tokens // tiles
    row = lax.broadcasted_iota(i32, (tiles, tiles), 0)
    column = lax.broadcasted_iota(i32, (tiles, tiles), 1)
    def upright(across):
        return jnp.sum(jnp.where(row == column, across, 0.0), axis=1, keepdims=True)

    clip_across = clip_ref[...].astype(f32)
    clip = upright(clip_across)
    length = upright(length_ref[...].astype(f32))
    rank = jnp.sum(
        jnp.where((clip == clip_across) & (column < row), 1.0, 0.0), axis=1, keepdims=True
    )
    off = clip.astype(i32) - g
    off = jnp.where(off < 0, off + groups, off)
    slot = jnp.where(off == 0, 0, jnp.where(off <= groups // 2, 2 * off - 1, 2 * (groups - off)))
    first = slot.astype(f32) * rs + rank * size
    part_of = lax.broadcasted_iota(i32, (tiles, tokens), 1) - size * lax.broadcasted_iota(
        i32, (tiles, tokens), 0
    )
    token = part_of.astype(f32)
    own = (part_of >= 0) & (part_of < size)
    at_row = jnp.sum(
        jnp.where(own & (token < length), first + token + 1.0, 0.0), axis=0, keepdims=True
    ) - 1.0
    hit = lax.broadcasted_iota(i32, (rows, tokens), 0) == at_row.astype(i32)
    select = jnp.where(hit, 1.0, 0.0).astype(jnp.bfloat16)
    placed = jnp.dot(select, cap_ref[...], preferred_element_type=f32).astype(jnp.bfloat16)
    stage[...] = placed
    x[pl.ds(0, rs), pl.ds(0, width)] = placed[:rs]
    flags = lax.dot_general(
        jnp.ones((16, tokens), jnp.bfloat16), select, (((1,), (1,)), ((), ())),
        preferred_element_type=f32,
    )
    blank = jnp.zeros((16, 128 - rs), f32)
    for p in range(groups):
        flag = jnp.concatenate([flags[:, p * rs:(p + 1) * rs], blank], axis=1).astype(jnp.bfloat16)
        if p:
            live_stage[p] = flag
        else:
            live[p] = flag

    pl.semaphore_wait(barrier, groups - 1 + 2)

    routes, flag_routes = [None], [None]
    for p in range(1, groups):
        part = pl.ds(p * rs, rs)
        to = (lax.rem(g + order[p], groups), m)
        routes.append(pltpu.make_async_remote_copy(
            src_ref=stage.at[part], dst_ref=x.at[part, pl.ds(0, width)], send_sem=z_send.at[p],
            recv_sem=z_recv.at[p], device_id=to, device_id_type=MESH))
        flag_routes.append(pltpu.make_async_remote_copy(
            src_ref=live_stage.at[p], dst_ref=live.at[p], send_sem=l_send.at[p],
            recv_sem=l_recv.at[p], device_id=to, device_id_type=MESH))

    chunk_rows = rows // chunks
    chunk_slots = groups // chunks

    def ring_copy(c, h, side):
        first, count = c * chunk_rows, chunk_rows
        if h == hops:
            count = chunk_rows // 2
            first = first + (count if side else 0)
        part = pl.ds(first, count)
        source = 0 if h == 1 else 2 * (h - 1) - 1 + side
        target = n - 1 if h == hops else 2 * h - 1 + side
        return pltpu.make_async_remote_copy(
            src_ref=x.at[part, pl.ds(source * width, width)],
            dst_ref=x.at[part, pl.ds(target * width, width)],
            send_sem=r_send.at[c, h - 1, side], recv_sem=r_recv.at[c, h - 1, side],
            device_id=(g, left if side else right), device_id_type=MESH)

    def hop(c, h):
        if h == 1:
            for p in range(c * chunk_slots, (c + 1) * chunk_slots):
                if p:
                    routes[p].wait_recv()
        else:
            ring_copy(c, h - 1, 0).wait_recv()
            ring_copy(c, h - 1, 1).wait_recv()
        ring_copy(c, h, 0).start()
        ring_copy(c, h, 1).start()

    half_rows = rows // halves
    half_chunks = chunks // halves
    tile = widest(cols, (1536, 768, 256, 128))
    seen = set()

    def project(part, f, count):
        for block in range(f, f + count):
            if block not in seen:
                seen.add(block)
                for c in weight_copies(block):
                    c.wait()
        if f + count == n:
            for c in both(part):
                ring_copy(c, hops, 0).wait_recv()
                ring_copy(c, hops, 1).wait_recv()
        depth = pl.ds(f * width, count * width)
        span = pl.ds(part * half_rows, half_rows)

        def body(j, carry):
            at = pl.ds(pl.multiple_of(j * tile, tile), tile)
            term = jnp.dot(x[span, depth], w[depth, at], preferred_element_type=jnp.float32)
            if f == 0:
                acc[span, at] = term
            else:
                acc[span, at] += term
            return carry

        lax.fori_loop(0, cols // tile, body, 0)

    for p in range(1, groups):
        if p == 1:
            ring_copy(0, 1, 0).start() if chunk_slots == 1 else None
            ring_copy(0, 1, 1).start() if chunk_slots == 1 else None
        routes[p].start()
        flag_routes[p].start()

    def both(part):
        return range(part * half_chunks, (part + 1) * half_chunks)

    early = [[(c, 1)] for c in both(0)] + [[] for _ in range(hops - 1)]
    for h in range(2, hops + 1):
        for c in both(0):
            early[c + h - 1].append((c, h))
    events = early[:half_chunks - 1]
    rest = early[half_chunks - 1:]
    events.append(rest[0] + [(0, 0)])
    for i in range(max(half_chunks, hops - 1)):
        event = []
        if i < half_chunks:
            event.append((half_chunks + i, 1))
        if i + 1 < len(rest):
            event += rest[i + 1]
        events.append(event + [(0, 0)] if i else event)
    for h in range(2, hops + 1):
        events.append([(c, h) for c in both(1)])

    pairs = [(f, 2) for f in range(1, n - 1, 2)]
    units = [(0, 0, 1)] + [(0, *pair) for pair in pairs] + [(0, n - 1, 1), (1, 0, 1)]
    units += [(1, *pair) for pair in pairs]
    begun = set()

    def ready(part, f, count):
        last = f + count - 1
        need = hops if last == n - 1 else (last + 1) // 2 + 1
        return all((c, need) in begun for c in both(part))

    for event in events:
        for c, h in event:
            if h == 0:
                if units and ready(*units[0]):
                    project(*units.pop(0))
                continue
            if not (c == 0 and h == 1 and chunk_slots == 1):
                hop(c, h)
            begun.add((c, h))
    while units:
        project(*units.pop(0))

    q_copy.wait()
    for p in range(1, groups):
        flag_routes[p].wait_recv()
    for c in both(1):
        ring_copy(c, hops, 0).wait_recv()
        ring_copy(c, hops, 1).wait_recv()

    flag_row = jnp.concatenate([live[p][0:1, :rs] for p in range(groups)], axis=1)
    bias = (flag_row.astype(f32) - 1.0) * 1e30
    factor = 1.4426950408889634 / HEAD_DIM**0.5
    q_rows = q.shape[0]
    q_tile = widest(q_rows, (512, 256, 128, 64))

    heads = head_cols // HEAD_DIM
    group_heads = widest(heads, (2, 1))
    wide = group_heads * HEAD_DIM
    done, last = pl.ds(0, half_rows), pl.ds(half_rows, half_rows)
    ones = jnp.ones((rows, HEAD_DIM), jnp.bfloat16)

    def finished(at):
        tail = acc[last, at] + jnp.dot(
            x[last, pl.ds((n - 1) * width, width)], w[pl.ds((n - 1) * width, width), at],
            preferred_element_type=f32,
        )
        return jnp.concatenate([acc[done, at].astype(jnp.bfloat16), tail.astype(jnp.bfloat16)], axis=0)

    def some_heads(i, carry):
        keys = finished(pl.ds(pl.multiple_of(i * wide, wide), wide))
        values = finished(pl.ds(pl.multiple_of(head_cols + i * wide, HEAD_DIM), wide))
        for j in range(group_heads):
            mine = slice(j * HEAD_DIM, (j + 1) * HEAD_DIM)
            col = pl.ds(pl.multiple_of(i * wide + j * HEAD_DIM, HEAD_DIM), HEAD_DIM)
            with_ones = jnp.concatenate([values[:, mine], ones], axis=1)
            for t in range(q_rows // q_tile):
                at = pl.ds(t * q_tile, q_tile)
                scores = lax.dot_general(
                    q[at, col], keys[:, mine], (((1,), (1,)), ((), ())), preferred_element_type=f32
                ) + bias
                top = jnp.max(scores, axis=1, keepdims=True)
                weights = jnp.exp2((scores - top) * factor).astype(jnp.bfloat16)
                total = jnp.dot(weights, with_ones, preferred_element_type=f32)
                out_ref[at, col] = (total[:, :HEAD_DIM] / total[:, HEAD_DIM:]).astype(out_ref.dtype)
        return carry

    lax.fori_loop(0, heads // group_heads, some_heads, 0)

    for p in range(1, groups):
        routes[p].wait_send()
        flag_routes[p].wait_send()
    for c in range(chunks):
        for h in range(1, hops + 1):
            for side in (0, 1):
                ring_copy(c, h, side).wait_send()


def local(captions, key_weight, value_weight, queries, tile_clip, tile_length):
    groups, n = lax.axis_size("group"), lax.axis_size("mp")
    tiles = tile_length.shape[0]
    tokens, width = captions.shape
    tile = tokens // tiles
    slots = max(2, 2 * tiles // groups)
    rs = -(-slots * tile // 16) * 16
    rows = groups * rs
    chunks, halves = min(groups, 8), 2
    head_cols = key_weight.shape[1]

    hops = n // 2
    bf = jnp.bfloat16
    vmem = pl.BlockSpec(memory_space=pltpu.VMEM)
    hbm = pl.BlockSpec(memory_space=pl.ANY)
    dma = pltpu.SemaphoreType.DMA
    return pl.pallas_call(
        functools.partial(kernel, groups, n, rs, chunks, halves),
        out_shape=jax.ShapeDtypeStruct(queries.shape, bf),
        in_specs=[vmem, vmem, vmem, hbm, hbm, hbm],
        out_specs=vmem,
        scratch_shapes=[
            pltpu.VMEM((rows, n * width), bf),
            pltpu.VMEM((n * width, 2 * head_cols), bf),
            pltpu.VMEM((rows, width), bf),
            pltpu.VMEM((groups, 16, 128), bf),
            pltpu.VMEM((groups, 16, 128), bf),
            pltpu.VMEM((rows, 2 * head_cols), jnp.float32),
            pltpu.VMEM(queries.shape, bf),
            dma((n, 2)), dma(()),
            dma((groups,)), dma((groups,)), dma((groups,)), dma((groups,)),
            dma((chunks, hops, 2)), dma((chunks, hops, 2)),
        ],
        compiler_params=pltpu.CompilerParams(
            collective_id=0, has_side_effects=True, vmem_limit_bytes=50 * 1024 * 1024
        ),
        cost_estimate=pl.CostEstimate(
            flops=4 * rows * n * width * head_cols + 4 * queries.size * rows,
            bytes_accessed=4 * key_weight.size + 4 * queries.size,
            transcendentals=queries.size * rows // HEAD_DIM,
        ),
    )(tile_clip.reshape(1, tiles), tile_length.reshape(1, tiles), captions, key_weight, value_weight, queries)


def solution(mesh):
    placed = (
        P("group", "mp"),
        P(None, "mp"),
        P(None, "mp"),
        P("group", "mp"),
        P("group", None),
        P("group"),
    )
    return jax.shard_map(
        local, mesh=mesh, in_specs=placed, out_specs=P("group", "mp"), check_vma=False
    )
```

```python
import functools

import jax
import jax.numpy as jnp
from jax import lax
from jax.experimental import pallas as pl
from jax.experimental.pallas import tpu as pltpu
from jax.sharding import PartitionSpec as P

HEAD_DIM = 128
MESH = pl.DeviceIdType.MESH


def ring_place(i, n):
    half = n // 2
    far = i // half
    return i * (1 - far) + far * (n + half - 1 - i)


def offsets_of(groups):
    order = [0]
    for k in range(1, groups // 2 + 1):
        order.append(k)
        if groups - k != k:
            order.append(groups - k)
    return order


def widest(total, options):
    return next(o for o in options if total % o == 0)


def kernel(
    groups, n, rs, chunks, halves,
    clip_hbm, length_hbm, cap_hbm, kw_ref, vw_ref, q_hbm, out_ref,
    x, w, stage, live_stage, live, acc, q,
    clip_ref, length_ref, cap_ref, in_sem, w_sem, q_sem, z_send, z_recv, l_send, l_recv, r_send, r_recv,
):
    g = lax.axis_index("group")
    m = lax.axis_index("mp")
    place = ring_place(m, n)
    right = ring_place(lax.rem(place + 1, n), n)
    left = ring_place(lax.rem(place + n - 1, n), n)
    rows, width = stage.shape
    head_cols = kw_ref.shape[1]
    cols = 2 * head_cols
    hops = n // 2
    order = offsets_of(groups)

    inputs = [
        pltpu.make_async_copy(clip_hbm, clip_ref, in_sem.at[0]),
        pltpu.make_async_copy(length_hbm, length_ref, in_sem.at[1]),
        pltpu.make_async_copy(cap_hbm, cap_ref, in_sem.at[2]),
    ]
    for c in inputs:
        c.start()

    def weight_copies(f):
        hop = (f + 1) // 2
        owner = ring_place(lax.rem(place + (n - hop if f % 2 else hop), n), n)
        part = pl.ds(pl.multiple_of(owner * width, width), width)
        return [
            pltpu.make_async_copy(kw_ref.at[part], w.at[pl.ds(f * width, width), pl.ds(0, head_cols)], w_sem.at[f, 0]),
            pltpu.make_async_copy(vw_ref.at[part], w.at[pl.ds(f * width, width), pl.ds(head_cols, head_cols)], w_sem.at[f, 1]),
        ]

    for f in range(n):
        for c in weight_copies(f):
            c.start()
    q_copy = pltpu.make_async_copy(q_hbm, q, q_sem)
    q_copy.start()

    barrier = pltpu.get_barrier_semaphore()
    for k in order[1:]:
        pl.semaphore_signal(barrier, inc=1, device_id=(lax.rem(g + k, groups), m), device_id_type=MESH)
    for side in (left, right):
        pl.semaphore_signal(barrier, inc=1, device_id=(g, side), device_id_type=MESH)

    for c in inputs:
        c.wait()
    f32, i32 = jnp.float32, jnp.int32
    tokens, tiles = cap_ref.shape[0], length_ref.shape[1]
    size = tokens // tiles
    row = lax.broadcasted_iota(i32, (tiles, tiles), 0)
    column = lax.broadcasted_iota(i32, (tiles, tiles), 1)
    def upright(across):
        return jnp.sum(jnp.where(row == column, across, 0.0), axis=1, keepdims=True)

    clip_across = clip_ref[...].astype(f32)
    clip = upright(clip_across)
    length = upright(length_ref[...].astype(f32))
    rank = jnp.sum(
        jnp.where((clip == clip_across) & (column < row), 1.0, 0.0), axis=1, keepdims=True
    )
    off = clip.astype(i32) - g
    off = jnp.where(off < 0, off + groups, off)
    slot = jnp.where(off == 0, 0, jnp.where(off <= groups // 2, 2 * off - 1, 2 * (groups - off)))
    first = slot.astype(f32) * rs + rank * size
    part_of = lax.broadcasted_iota(i32, (tiles, tokens), 1) - size * lax.broadcasted_iota(
        i32, (tiles, tokens), 0
    )
    token = part_of.astype(f32)
    own = (part_of >= 0) & (part_of < size)
    at_row = jnp.sum(
        jnp.where(own & (token < length), first + token + 1.0, 0.0), axis=0, keepdims=True
    ) - 1.0
    hit = lax.broadcasted_iota(i32, (rows, tokens), 0) == at_row.astype(i32)
    select = jnp.where(hit, 1.0, 0.0).astype(jnp.bfloat16)
    placed = jnp.dot(select, cap_ref[...], preferred_element_type=f32).astype(jnp.bfloat16)
    stage[...] = placed
    x[pl.ds(0, rs), pl.ds(0, width)] = placed[:rs]
    flags = lax.dot_general(
        jnp.ones((16, tokens), jnp.bfloat16), select, (((1,), (1,)), ((), ())),
        preferred_element_type=f32,
    )
    blank = jnp.zeros((16, 128 - rs), f32)
    for p in range(groups):
        flag = jnp.concatenate([flags[:, p * rs:(p + 1) * rs], blank], axis=1).astype(jnp.bfloat16)
        if p:
            live_stage[p] = flag
        else:
            live[p] = flag

    pl.semaphore_wait(barrier, groups - 1 + 2)

    routes, flag_routes = [None], [None]
    for p in range(1, groups):
        part = pl.ds(p * rs, rs)
        to = (lax.rem(g + order[p], groups), m)
        routes.append(pltpu.make_async_remote_copy(
            src_ref=stage.at[part], dst_ref=x.at[part, pl.ds(0, width)], send_sem=z_send.at[p],
            recv_sem=z_recv.at[p], device_id=to, device_id_type=MESH))
        flag_routes.append(pltpu.make_async_remote_copy(
            src_ref=live_stage.at[p], dst_ref=live.at[p], send_sem=l_send.at[p],
            recv_sem=l_recv.at[p], device_id=to, device_id_type=MESH))

    chunk_rows = rows // chunks
    chunk_slots = groups // chunks

    def ring_copy(c, h, side):
        first, count = c * chunk_rows, chunk_rows
        if h == hops:
            count = chunk_rows // 2
            first = first + (count if side else 0)
        part = pl.ds(first, count)
        source = 0 if h == 1 else 2 * (h - 1) - 1 + side
        target = n - 1 if h == hops else 2 * h - 1 + side
        return pltpu.make_async_remote_copy(
            src_ref=x.at[part, pl.ds(source * width, width)],
            dst_ref=x.at[part, pl.ds(target * width, width)],
            send_sem=r_send.at[c, h - 1, side], recv_sem=r_recv.at[c, h - 1, side],
            device_id=(g, left if side else right), device_id_type=MESH)

    def hop(c, h):
        if h == 1:
            for p in range(c * chunk_slots, (c + 1) * chunk_slots):
                if p:
                    routes[p].wait_recv()
        else:
            ring_copy(c, h - 1, 0).wait_recv()
            ring_copy(c, h - 1, 1).wait_recv()
        ring_copy(c, h, 0).start()
        ring_copy(c, h, 1).start()

    half_rows = rows // halves
    half_chunks = chunks // halves
    tile = widest(cols, (1536, 768, 256, 128))
    seen = set()

    def project(part, f, count):
        for block in range(f, f + count):
            if block not in seen:
                seen.add(block)
                for c in weight_copies(block):
                    c.wait()
        if f + count == n:
            for c in both(part):
                ring_copy(c, hops, 0).wait_recv()
                ring_copy(c, hops, 1).wait_recv()
        depth = pl.ds(f * width, count * width)
        span = pl.ds(part * half_rows, half_rows)

        def body(j, carry):
            at = pl.ds(pl.multiple_of(j * tile, tile), tile)
            term = jnp.dot(x[span, depth], w[depth, at], preferred_element_type=jnp.float32)
            if f == 0:
                acc[span, at] = term
            else:
                acc[span, at] += term
            return carry

        lax.fori_loop(0, cols // tile, body, 0)

    for p in range(1, groups):
        if p == 1:
            ring_copy(0, 1, 0).start() if chunk_slots == 1 else None
            ring_copy(0, 1, 1).start() if chunk_slots == 1 else None
        routes[p].start()
        flag_routes[p].start()

    def both(part):
        return range(part * half_chunks, (part + 1) * half_chunks)

    early = [[(c, 1)] for c in both(0)] + [[] for _ in range(hops - 1)]
    for h in range(2, hops + 1):
        for c in both(0):
            early[c + h - 1].append((c, h))
    events = early[:half_chunks - 1]
    rest = early[half_chunks - 1:]
    events.append(rest[0] + [(0, 0)])
    for i in range(max(half_chunks, hops - 1)):
        event = []
        if i < half_chunks:
            event.append((half_chunks + i, 1))
        if i + 1 < len(rest):
            event += rest[i + 1]
        events.append(event + [(0, 0)] if i else event)
    for h in range(2, hops + 1):
        events.append([(c, h) for c in both(1)])

    pairs = [(f, 2) for f in range(1, n - 1, 2)]
    units = [(0, 0, 1)] + [(0, *pair) for pair in pairs] + [(0, n - 1, 1), (1, 0, 1)]
    units += [(1, *pair) for pair in pairs]
    begun = set()

    def ready(part, f, count):
        last = f + count - 1
        need = hops if last == n - 1 else (last + 1) // 2 + 1
        return all((c, need) in begun for c in both(part))

    for event in events:
        for c, h in event:
            if h == 0:
                if units and ready(*units[0]):
                    project(*units.pop(0))
                continue
            if not (c == 0 and h == 1 and chunk_slots == 1):
                hop(c, h)
            begun.add((c, h))
    while units:
        project(*units.pop(0))

    q_copy.wait()
    for p in range(1, groups):
        flag_routes[p].wait_recv()
    for c in both(1):
        ring_copy(c, hops, 0).wait_recv()
        ring_copy(c, hops, 1).wait_recv()

    flag_row = jnp.concatenate([live[p][0:1, :rs] for p in range(groups)], axis=1)
    bias = (flag_row.astype(f32) - 1.0) * 1e30
    factor = 1.4426950408889634 / HEAD_DIM**0.5
    q_rows = q.shape[0]
    q_tile = widest(q_rows, (512, 256, 128, 64))

    heads = head_cols // HEAD_DIM
    group_heads = widest(heads, (2, 1))
    wide = group_heads * HEAD_DIM
    done, last = pl.ds(0, half_rows), pl.ds(half_rows, half_rows)
    ones = jnp.ones((rows, HEAD_DIM), jnp.bfloat16)

    def finished(at):
        tail = acc[last, at] + jnp.dot(
            x[last, pl.ds((n - 1) * width, width)], w[pl.ds((n - 1) * width, width), at],
            preferred_element_type=f32,
        )
        return jnp.concatenate([acc[done, at].astype(jnp.bfloat16), tail.astype(jnp.bfloat16)], axis=0)

    def some_heads(i, carry):
        keys = finished(pl.ds(pl.multiple_of(i * wide, wide), wide))
        values = finished(pl.ds(pl.multiple_of(head_cols + i * wide, HEAD_DIM), wide))
        for j in range(group_heads):
            mine = slice(j * HEAD_DIM, (j + 1) * HEAD_DIM)
            col = pl.ds(pl.multiple_of(i * wide + j * HEAD_DIM, HEAD_DIM), HEAD_DIM)
            with_ones = jnp.concatenate([values[:, mine], ones], axis=1)
            for t in range(q_rows // q_tile):
                at = pl.ds(t * q_tile, q_tile)
                scores = lax.dot_general(
                    q[at, col], keys[:, mine], (((1,), (1,)), ((), ())), preferred_element_type=f32
                ) + bias
                top = jnp.max(scores, axis=1, keepdims=True)
                weights = jnp.exp2((scores - top) * factor).astype(jnp.bfloat16)
                total = jnp.dot(weights, with_ones, preferred_element_type=f32)
                out_ref[at, col] = (total[:, :HEAD_DIM] / total[:, HEAD_DIM:]).astype(out_ref.dtype)
        return carry

    lax.fori_loop(0, heads // group_heads, some_heads, 0)

    for p in range(1, groups):
        routes[p].wait_send()
        flag_routes[p].wait_send()
    for c in range(chunks):
        for h in range(1, hops + 1):
            for side in (0, 1):
                ring_copy(c, h, side).wait_send()


def local(captions, key_weight, value_weight, queries, tile_clip, tile_length):
    groups, n = lax.axis_size("group"), lax.axis_size("mp")
    tiles = tile_length.shape[0]
    tokens, width = captions.shape
    tile = tokens // tiles
    slots = max(2, 2 * tiles // groups)
    rs = -(-slots * tile // 16) * 16
    rows = groups * rs
    chunks, halves = min(groups, 8), 2
    head_cols = key_weight.shape[1]

    hops = n // 2
    bf = jnp.bfloat16
    vmem = pl.BlockSpec(memory_space=pltpu.VMEM)
    hbm = pl.BlockSpec(memory_space=pltpu.HBM)
    dma = pltpu.SemaphoreType.DMA
    return pl.pallas_call(
        functools.partial(kernel, groups, n, rs, chunks, halves),
        out_shape=jax.ShapeDtypeStruct(queries.shape, bf),
        in_specs=[hbm] * 6,
        out_specs=vmem,
        scratch_shapes=[
            pltpu.VMEM((rows, n * width), bf),
            pltpu.VMEM((n * width, 2 * head_cols), bf),
            pltpu.VMEM((rows, width), bf),
            pltpu.VMEM((groups, 16, 128), bf),
            pltpu.VMEM((groups, 16, 128), bf),
            pltpu.VMEM((rows, 2 * head_cols), jnp.float32),
            pltpu.VMEM(queries.shape, bf),
            pltpu.VMEM((1, tiles), jnp.int32),
            pltpu.VMEM((1, tiles), jnp.int32),
            pltpu.VMEM(captions.shape, bf),
            dma((3,)), dma((n, 2)), dma(()),
            dma((groups,)), dma((groups,)), dma((groups,)), dma((groups,)),
            dma((chunks, hops, 2)), dma((chunks, hops, 2)),
        ],
        compiler_params=pltpu.CompilerParams(
            collective_id=0, has_side_effects=True, vmem_limit_bytes=58 * 1024 * 1024
        ),
        cost_estimate=pl.CostEstimate(
            flops=4 * rows * n * width * head_cols + 4 * queries.size * rows,
            bytes_accessed=4 * key_weight.size + 4 * queries.size,
            transcendentals=queries.size * rows // HEAD_DIM,
        ),
    )(tile_clip.reshape(1, tiles), tile_length.reshape(1, tiles), captions, key_weight, value_weight, queries)


def solution(mesh):
    placed = (
        P("group", "mp"),
        P(None, "mp"),
        P(None, "mp"),
        P("group", "mp"),
        P("group", None),
        P("group"),
    )
    return jax.shard_map(
        local, mesh=mesh, in_specs=placed, out_specs=P("group", "mp"), check_vma=False
    )
```
